32 devices in a mesh: band: 2 (over y), exp: 16 (over z, x, core).
Axes of the slice: x: 2, y: 2, z: 4, core: 2. Of those that a mesh axis runs over, the one named last changes fastest.
Arguments:
- exposure: float32 [32768, 512], P(('band', 'exp')), parts along dimension 0, may hold values from -8 to 8, as said below
- psf_taps: bfloat16 [32, 15], P(('band', 'exp')), parts along dimension 0, may hold values from -1.5 to 1.5
- col_warp: bfloat16 [16384, 512], P(('band', 'exp')), parts along dimension 0, may hold values from -0.25 to 0.25
- row_warp: bfloat16 [16384, 1024], P(('band', 'exp')), parts along dimension 0, may hold values from -0.1875 to 0.1875
- row_patch: int32 [16384, 1], P(('band', 'exp')), parts along dimension 0, may hold values from 0 to 15; in each aligned block of 512 rows (0 to 511, 512 to 1023, ...) at most 64 rows name the same one
- row_prow: int32 [16384], P(('band', 'exp')), parts along dimension 0, may hold values from 0 to 31
- owner_map: int32 [32], P('band'), parts along dimension 0, may hold values from 0 to 15, each once
Outputs:
- coadd: float32 [1024, 512], P(('band', 'exp')), parts along dimension 0
The draws below stay inside these ranges and needn't reach their ends.
There are 2 independent parts, one for each index of `band`. The reference program is written for one: setup_inputs(seed, part) draws one part's arguments, and reference() takes and returns one part's arrays. A program takes and returns all parts, laid end to end along the dimension named above; each array names one. Nothing has to cross between parts.
Inputs may be any that keep to these rules, and one draw needn't show every extreme that they name: `row_patch`: the 512 resampled rows of one exposure piece (aligned blocks) name any one patch at most 64 times, a bound that some block reaches. `exposure`: each piece carries a background level per block of 128 columns on top of the sky noise.
All inputs are finite; a program needn't handle non-finite values.
Results may differ from the reference program's by a relative error of at most 0.0051.
Values sent between devices are 32-bit elements; how exact they have to be, the bound alone decides.
No kernel may reach another device: no remote copies, remote signals or barrier semaphores. Data moves between devices by JAX's collectives and lax.ppermute only.
A program may use at most 64 MiB of HBM per device.

```python
import math
import jax
import jax.numpy as jnp
import numpy as np
from jax import lax

W = 512
R = 1024
STRIP = 16
TAPS = 15
PATCH_ROWS = 32
RO = 512
EXPOSURES = 16
NPATCH = 16
ROWS = 16384
OUT_ROWS = 8192
CAP = 64


def draw_exposure(key, part):
    noise_key, level_key = jax.random.split(jax.random.fold_in(key, 11))
    noise = jnp.clip(jax.random.normal(noise_key, (ROWS, W), jnp.float32), -5.0, 5.0)
    levels = jax.random.uniform(level_key, (EXPOSURES, W // 128), jnp.float32, -2.0, 2.0)
    full = jnp.repeat(jnp.repeat(levels, 128, axis=1), R, axis=0)
    return noise + full


def with_ends(values, stream_key, low, top_value):
    longest = values.shape.index(max(values.shape))
    spots = []
    for shift in (0, 1):
        where = [jax.random.randint(jax.random.fold_in(stream_key, axis), (), 0, length) for axis, length in enumerate(values.shape)]
        where[longest] = (where[longest] + shift) % values.shape[longest]
        spots.append(tuple(where))
    return values.at[spots[0]].set(low).at[spots[1]].set(top_value)


def block_levels(stream_key, dims, shards, least, high):
    def one(axis_at, blocks):
        draws = jax.random.uniform(jax.random.fold_in(jax.random.fold_in(stream_key, 6), axis_at), (blocks,), jnp.float32, least / len(shards), high / len(shards))
        return jnp.repeat(jnp.exp(draws), dims[axis_at] // blocks).reshape((-1,) + (1,) * (len(dims) - axis_at - 1))

    level = one(*shards[0])
    for cut in shards[1:]:
        level = level * one(*cut)
    return level


def assign_block(stream_key, own, number, rows, amount, top, most, skew):
    ranking = jax.random.permutation(stream_key, amount)
    packed, usual = shares(amount, rows * top, most, skew, True), shares(amount, rows * top, most, skew, False)
    places = jnp.arange(amount)

    def named(tallies, turn):
        used = int((tallies > 0).sum())
        fixed = max(1, used // 4)
        passed = fixed + (places - fixed + turn * (used - fixed)) % max(1, amount - fixed)
        return jnp.zeros((amount,), jnp.int32).at[ranking[jnp.where(places < fixed, places, passed)]].set(jnp.asarray(tallies, jnp.int32))

    tallies = jnp.where(number % 4 == 0, named(packed, number // 4), named(usual, number - number // 4 - 1))
    mixed = jax.random.permutation(jax.random.fold_in(own, 3), amount)
    source_of, taker = mixed[0:amount // 2 * 2:2], mixed[1:amount // 2 * 2:2]
    room = jnp.minimum(tallies[source_of] - 1, most - tallies[taker]) // 2
    room = jnp.where((source_of == ranking[0]) | (taker == ranking[0]) | (tallies[taker] == 0), 0, jnp.maximum(room, 0))
    passed = jax.random.randint(jax.random.fold_in(own, 4), (amount // 2,), 0, 1 << 20) % (room + 1)
    tallies = tallies.at[source_of].add(-passed).at[taker].add(passed)
    labels = jnp.searchsorted(jnp.cumsum(tallies), jnp.arange(rows * top), side="right").astype(jnp.int32)
    listing = labels.reshape(top, rows).T
    listing = listing[jax.random.permutation(jax.random.fold_in(own, 1), rows)]
    turn = jax.random.randint(jax.random.fold_in(own, 2), (rows, 1), 0, top)
    return jnp.take_along_axis(listing, (jnp.arange(top)[None, :] + turn) % top, axis=1)


def shares(count, total, limit, lean, full):
    weights = [(1 << 20) // math.isqrt(rank ** lean) + 1 for rank in range(1, count + 1)]
    largest = limit if full else min(limit, max(-(-total // count), total * weights[0] // sum(weights)))
    least = 1 if total - largest >= count - 1 else 0
    holding, rest = [largest] + [least] * (count - 1), total - largest - least * (count - 1)
    while rest > 0:
        movable = [i for i in range(1, count) if holding[i] < largest] or [i for i in range(1, count) if holding[i] < limit]
        mass, left = sum([weights[i] for i in movable]), rest
        for i in movable:
            extra = min(limit - holding[i], max(1, left * weights[i] // mass), rest)
            holding[i] = holding[i] + extra
            rest = rest - extra
    return np.array(holding)


def bell_draw(own_key, extent, scale, reach, cuts=(), kind=jnp.bfloat16):
    entries = jax.random.normal(own_key, extent, jnp.float32) * scale
    if len(cuts) > 0:
        entries = block_levels(own_key, extent, cuts, -0.22, 0.18) * entries
    return jnp.clip(entries, min=-reach, max=reach).astype(kind)


def setup_inputs(seed: int = 0, part: int = 0) -> dict:
    streams_of = jax.random.split(jax.random.key(seed), 8)
    part_keys = jax.random.split(jax.random.fold_in(streams_of[7], part), 8)
    exposure = draw_exposure(jax.random.fold_in(jax.random.fold_in(streams_of[7], part), 71), part)
    psf_taps = bell_draw(part_keys[1], (EXPOSURES, TAPS), 0.25, 1.5, ((0, 16),))
    col_warp = bell_draw(part_keys[2], (EXPOSURES * W, W), W ** -0.5, 0.25, ((0, 16),))
    row_warp = bell_draw(part_keys[3], (OUT_ROWS, R), R ** -0.5, 0.1875, ((0, 16),))
    row_patch_keys = jax.random.split(jax.random.fold_in(part_keys[4], 1), OUT_ROWS // RO)
    row_patch_turns = jax.random.permutation(jax.random.fold_in(part_keys[4], 3), OUT_ROWS // RO)
    row_patch = jax.vmap(lambda own, number: assign_block(jax.random.fold_in(part_keys[4], 2), own, number, RO, NPATCH, 1, CAP, 2))(row_patch_keys, row_patch_turns).reshape((OUT_ROWS, 1))
    row_prow = with_ends(jax.random.randint(part_keys[5], (OUT_ROWS,), 0, PATCH_ROWS), jax.random.fold_in(part_keys[5], 1), 0, PATCH_ROWS - 1).astype(jnp.int32)
    owner_map = jax.random.permutation(part_keys[6], NPATCH).astype(jnp.int32)
    return {"exposure": exposure, "psf_taps": psf_taps, "col_warp": col_warp, "row_warp": row_warp, "row_patch": row_patch, "row_prow": row_prow, "owner_map": owner_map}


def make_band(taps, width):
    half = (TAPS - 1) // 2
    rows_idx = jnp.arange(width, dtype=jnp.int32)[:, None]
    cols_idx = jnp.arange(width, dtype=jnp.int32)[None, :]
    offset = rows_idx - cols_idx + half
    band = jnp.zeros((width, width), jnp.bfloat16)
    for tap in range(TAPS):
        band = jnp.where(offset == tap, taps[tap], band)
    return band


def reference(exposure, psf_taps, col_warp, row_warp, row_patch, row_prow, owner_map):
    pieces = exposure.reshape(EXPOSURES, R, W)
    first = pieces[:, :STRIP]
    last = pieces[:, R - STRIP:]
    diff = last - jnp.roll(first, -1, axis=0)
    off_next = jnp.mean(diff.reshape(EXPOSURES, STRIP, W // 128, 128), axis=(1, 3))
    off_prev = jnp.roll(off_next, 1, axis=0)
    shift = jnp.repeat(-0.5 * off_next + 0.5 * off_prev, 128, axis=1)
    corrected = (pieces + shift[:, None, :]).astype(jnp.bfloat16)
    cw = col_warp.reshape(EXPOSURES, W, W)
    rw = row_warp.reshape(EXPOSURES, RO, R)

    def one_piece(items):
        image, taps, colw, roww = items
        band = make_band(taps, W)
        matched = jnp.dot(image, band, preferred_element_type=jnp.float32).astype(jnp.bfloat16)
        warped_cols = jnp.dot(matched, colw, preferred_element_type=jnp.float32).astype(jnp.bfloat16)
        return jnp.dot(roww, warped_cols, preferred_element_type=jnp.float32)

    warped = lax.map(one_piece, (corrected, psf_taps, cw, rw)).reshape(OUT_ROWS, W)
    slot_of = jnp.zeros((NPATCH,), jnp.int32).at[owner_map].set(jnp.arange(NPATCH, dtype=jnp.int32))
    key = slot_of[row_patch[:, 0]] * PATCH_ROWS + row_prow
    sums = jax.ops.segment_sum(warped, key, num_segments=NPATCH * PATCH_ROWS)
    counts = jax.ops.segment_sum(jnp.ones((OUT_ROWS,), jnp.float32), key, num_segments=NPATCH * PATCH_ROWS)
    return sums / jnp.maximum(counts, 1.0)[:, None]
```

```python
import functools

import jax
import jax.numpy as jnp
from jax import lax
from jax.experimental import pallas as pl
from jax.experimental.pallas import tpu as pltpu
from jax.sharding import PartitionSpec as P

STRIP = 16
TAPS = 15
PATCH_ROWS = 32
LANES = 128
SUB = 8
CHUNKS = 4
QUAD = 4
VMEM_LIMIT = 48 * 1024 * 1024

f32 = jnp.float32
bf16 = jnp.bfloat16


def swap(block, mask, count):
    return lax.ppermute(block, "exp", [(i, i ^ mask) for i in range(count)])


def swap_ring(block, count):
    pairs = [((2 * i + 1) % count, (2 * i + 2) % count) for i in range(count // 2)]
    return lax.ppermute(block, "exp", pairs + [(b, a) for a, b in pairs])


def call(body, outs, ins, args, scratch=(), flops=0, **more):
    moved = sum(a.size * a.dtype.itemsize for a in args)
    return pl.pallas_call(
        body,
        out_shape=outs,
        in_specs=ins,
        out_specs=jax.tree.map(lambda _: pl.BlockSpec(memory_space=pltpu.VMEM), outs),
        scratch_shapes=scratch,
        compiler_params=pltpu.CompilerParams(vmem_limit_bytes=VMEM_LIMIT),
        cost_estimate=pl.CostEstimate(flops=flops, bytes_accessed=moved, transcendentals=0),
        **more,
    )(*args)


def strips_body(first_ref, last_ref, pair_ref, ring_ref, own_ref):
    even = lax.rem(lax.axis_index("exp"), 2) == 0
    own_ref[...] = jnp.zeros_like(own_ref)
    pair_ref[...] = jnp.zeros_like(pair_ref)
    ring_ref[...] = jnp.zeros_like(ring_ref)
    scale = 1.0 / (STRIP * LANES)
    for b in range(first_ref.shape[1] // LANES):
        at = slice(b * LANES, (b + 1) * LANES)
        means = []
        for ref in (first_ref, last_ref):
            column = jnp.sum(ref[:, at], axis=0, keepdims=True)
            total = jnp.sum(column, axis=1, keepdims=True)
            means.append(jnp.broadcast_to(total * scale, (1, LANES)))
        first, last = means
        own_ref[b : b + 1] = 0.5 * (first + last)
        pair_ref[b : b + 1] = jnp.where(even, last, first)
        ring_ref[b : b + 1] = jnp.where(even, first, last)


def local_body(
    owner_ref, taps_ref, patch_ref, prow_ref, own_ref, exposure, col_warp, row_warp,
    sums_ref, rows_ref, count_ref, blocks_ref,
    image, cols, rows, band, merged, warped, high, low, select, sems,
):
    count = owner_ref.shape[0]
    height, width = exposure.shape
    nb = width // LANES
    step = height // CHUNKS
    copies = [pltpu.make_async_copy(col_warp, cols, sems.at[0])]
    for i in range(CHUNKS):
        at = pl.ds(i * step, step)
        copies.append(pltpu.make_async_copy(exposure.at[at], image.at[at], sems.at[1 + i]))
    copies.append(pltpu.make_async_copy(row_warp, rows, sems.at[1 + CHUNKS]))
    for copy in copies:
        copy.start()

    delta = lax.broadcasted_iota(jnp.int32, (LANES, LANES), 0) - lax.broadcasted_iota(
        jnp.int32, (LANES, LANES), 1
    )
    tiles = {}
    for side in (-1, 0, 1):
        offset = delta + side * LANES + (TAPS - 1) // 2
        tile = jnp.zeros((LANES, LANES), f32)
        for tap in range(TAPS):
            tile = jnp.where(offset == tap, taps_ref[0:1, tap : tap + 1].astype(f32), tile)
        tiles[side] = tile.astype(bf16)
    for i in range(nb):
        for k in range(nb):
            tile = tiles.get(i - k, jnp.zeros((LANES, LANES), bf16))
            band[i * LANES : (i + 1) * LANES, k * LANES : (k + 1) * LANES] = tile

    me = lax.axis_index("exp")
    patch = patch_ref[...]
    slot = jnp.zeros_like(patch)
    for k in range(count):
        mask = me ^ k
        place = (mask & 1) * (count // 2) + lax.shift_right_logical(mask, 1)
        slot = jnp.where(patch == owner_ref[k], place, slot)
    key = slot * PATCH_ROWS + prow_ref[...]
    slots = lax.broadcasted_iota(jnp.int32, select.shape, 0)
    select[...] = jnp.where(slots == key, 1.0, 0.0).astype(bf16)

    ones = jnp.ones((select.shape[1], LANES), bf16)
    held = jnp.dot(select[...], ones, preferred_element_type=f32)
    lane = lax.broadcasted_iota(jnp.int32, (SUB, LANES), 1)
    for j in range(count):
        tile = jnp.zeros((SUB, LANES), f32)
        for s in range(PATCH_ROWS // SUB):
            at = j * PATCH_ROWS + s * SUB
            tile = jnp.where(lane == s, held[at : at + SUB], tile)
        count_ref[j * SUB : (j + 1) * SUB] = tile

    copies[0].wait()
    both = jnp.dot(band[...], cols[...], preferred_element_type=f32)
    blocks_ref[...] = jnp.zeros_like(blocks_ref)
    for b in range(nb):
        part = both[b * LANES : (b + 1) * LANES]
        blocks_ref[b : b + 1] = jnp.sum(part, axis=0, keepdims=True)
    merged[...] = both.astype(bf16)

    warped[:, width:] = jnp.ones((height, LANES), bf16)
    for i in range(CHUNKS):
        copies[1 + i].wait()
        at = slice(i * step, (i + 1) * step)
        parts = []
        for b in range(nb):
            piece = image[at, b * LANES : (b + 1) * LANES] - own_ref[b : b + 1]
            parts.append(piece.astype(bf16))
        centred = jnp.concatenate(parts, axis=1)
        warped[at, :width] = jnp.dot(
            centred, merged[...], preferred_element_type=f32
        ).astype(bf16)
    copies[1 + CHUNKS].wait()
    values = jnp.dot(rows[...], warped[...], preferred_element_type=f32)
    top = values.astype(bf16)
    high[...] = top
    low[...] = (values - top.astype(f32)).astype(bf16)
    sums = jnp.dot(select[...], high[...], preferred_element_type=f32) + jnp.dot(
        select[...], low[...], preferred_element_type=f32
    )
    sums_ref[...] = sums[:, :width]
    rows_ref[...] = sums[:, width:]


def level_rows(pair_ref, ring_ref, blocks_ref):
    nb = blocks_ref.shape[1] // LANES
    out = []
    for c in range(nb):
        total = jnp.zeros((1, LANES), f32)
        for b in range(nb):
            level = 0.5 * (pair_ref[b : b + 1] + ring_ref[b : b + 1])
            total += level * blocks_ref[b : b + 1, c * LANES : (c + 1) * LANES]
        out.append(total)
    return out


def send_body(pair_ref, ring_ref, blocks_ref, sums_ref, rows_ref, count_ref, out_ref):
    level = level_rows(pair_ref, ring_ref, blocks_ref)
    half = count_ref.shape[0] // SUB // 2
    size = out_ref.shape[0] // half
    for j in range(half):
        at = (half + j) * PATCH_ROWS
        weight = rows_ref[at : at + PATCH_ROWS]
        for c, row in enumerate(level):
            to = j * size + c * PATCH_ROWS
            part = sums_ref[at : at + PATCH_ROWS, c * LANES : (c + 1) * LANES]
            out_ref[to : to + PATCH_ROWS] = part + weight * row
        to = j * size + len(level) * PATCH_ROWS
        out_ref[to : to + SUB] = count_ref[(half + j) * SUB : (half + j + 1) * SUB]


def merge_body(
    pair_ref, ring_ref, blocks_ref, sums_ref, rows_ref, count_ref, got_ref, *out_refs
):
    level = level_rows(pair_ref, ring_ref, blocks_ref)
    half = count_ref.shape[0] // SUB // 2
    size = got_ref.shape[0] // half
    for j in range(half):
        quad, far = j % QUAD, j // QUAD
        ref = out_refs[quad] if far == 0 else out_refs[QUAD + quad]
        base = 0 if far == 0 else (far - 1) * size
        at = j * PATCH_ROWS
        weight = rows_ref[at : at + PATCH_ROWS]
        for c, row in enumerate(level):
            to = c * PATCH_ROWS
            part = sums_ref[at : at + PATCH_ROWS, c * LANES : (c + 1) * LANES]
            got = got_ref[j * size + to : j * size + to + PATCH_ROWS]
            ref[base + to : base + to + PATCH_ROWS] = part + weight * row + got
        to = len(level) * PATCH_ROWS
        got = got_ref[j * size + to : j * size + to + SUB]
        ref[base + to : base + to + SUB] = count_ref[j * SUB : (j + 1) * SUB] + got


def far_body(a_ref, b_ref, c_ref, d_ref, *out_refs):
    size = out_refs[0].shape[0]
    for i, ref in enumerate(out_refs):
        at = slice(i * size, (i + 1) * size)
        ref[...] = (a_ref[at] + b_ref[at]) + (c_ref[at] + d_ref[at])


def final_body(*refs):
    out_ref = refs[-1]
    total = refs[0][...]
    for ref in refs[1:-1]:
        total = total + ref[...]
    nb = out_ref.shape[1] // LANES
    held = total[nb * PATCH_ROWS :]
    for s in range(PATCH_ROWS // SUB):
        number = jnp.maximum(held[:, s : s + 1], 1.0)
        for c in range(nb):
            at = c * PATCH_ROWS + s * SUB
            out_ref[s * SUB : (s + 1) * SUB, c * LANES : (c + 1) * LANES] = (
                total[at : at + SUB] / number
            )


def on_device(exposure, psf_taps, col_warp, row_warp, row_patch, row_prow, owner_map):
    height, width = exposure.shape
    out_rows = row_warp.shape[0]
    count = lax.axis_size("exp")
    nb = width // LANES
    slots = count * PATCH_ROWS
    half, high_groups = count // 2, count // (2 * QUAD)
    size = PATCH_ROWS * nb + SUB
    vmem = pl.BlockSpec(memory_space=pltpu.VMEM)
    smem = pl.BlockSpec(memory_space=pltpu.SMEM)
    anywhere = pl.BlockSpec(memory_space=pl.ANY)

    def shape(*dims):
        return jax.ShapeDtypeStruct(dims, f32)

    tile = shape(-(-nb // SUB) * SUB, LANES)
    pair, ring, own = pl.pallas_call(
        strips_body,
        grid=(1,),
        out_shape=[tile, tile, tile],
        in_specs=[
            pl.BlockSpec((STRIP, width), lambda i: (0, 0)),
            pl.BlockSpec((STRIP, width), lambda i: (height // STRIP - 1, 0)),
        ],
        out_specs=[pl.BlockSpec(tile.shape, lambda i: (0, 0))] * 3,
    )(exposure, exposure)
    pair = swap(pair, 1, count)
    ring = swap_ring(ring, count)

    wide = width + LANES
    sums, rows, held, blocks = call(
        local_body,
        [shape(slots, width), shape(slots, LANES), shape(count * SUB, LANES),
         shape(tile.shape[0], width)],
        [smem, vmem, vmem, vmem, vmem, anywhere, anywhere, anywhere],
        (owner_map, psf_taps, row_patch.reshape(1, out_rows), row_prow.reshape(1, out_rows),
         own, exposure, col_warp, row_warp),
        scratch=[
            pltpu.VMEM((height, width), f32),
            pltpu.VMEM((width, width), bf16),
            pltpu.VMEM((out_rows, height), bf16),
            pltpu.VMEM((width, width), bf16),
            pltpu.VMEM((width, width), bf16),
            pltpu.VMEM((height, wide), bf16),
            pltpu.VMEM((out_rows, wide), bf16),
            pltpu.VMEM((out_rows, wide), bf16),
            pltpu.VMEM((slots, out_rows), bf16),
            pltpu.SemaphoreType.DMA((CHUNKS + 2,)),
        ],
        flops=2 * height * width * (width + out_rows) + 4 * slots * out_rows * width,
    )
    common = (pair, ring, blocks, sums, rows, held)
    send = call(send_body, shape(half * size, LANES), [vmem] * 6, common)
    got = swap(send, 1, count)

    shapes = [shape(size, LANES)] * QUAD
    if high_groups > 1:
        shapes += [shape((high_groups - 1) * size, LANES)] * QUAD
    parts = call(merge_body, shapes, [vmem] * 7, common + (got,))
    near, far = parts[:QUAD], parts[QUAD:]
    terms = [near[0]]
    if high_groups > 1:
        far = [far[0]] + [swap(far[q], 2 * q, count) for q in range(QUAD - 1, 0, -1)]
    near_got = [swap(near[q], 2 * q, count) for q in range(QUAD - 1, 0, -1)]
    if high_groups > 1:
        sent = call(far_body, [shape(size, LANES)] * (high_groups - 1), [vmem] * QUAD, far)
        terms += [swap(sent[h - 1], 2 * QUAD * h, count) for h in range(1, high_groups)]
    terms += near_got
    return call(final_body, shape(PATCH_ROWS, width), [vmem] * len(terms), tuple(terms))


def solution(mesh):
    placed = (
        P(("band", "exp"), None),
        P(("band", "exp"), None),
        P(("band", "exp"), None),
        P(("band", "exp"), None),
        P(("band", "exp"), None),
        P(("band", "exp")),
        P("band"),
    )
    return jax.shard_map(
        on_device, mesh=mesh, in_specs=placed, out_specs=P(("band", "exp"), None), check_vma=False
    )
```

```python
import jax
import jax.numpy as jnp
from jax import lax
from jax.experimental import pallas as pl
from jax.experimental.pallas import tpu as pltpu
from jax.sharding import PartitionSpec as P

STRIP = 16
TAPS = 15
PATCH_ROWS = 32
LANES = 128
SUB = 8
CHUNKS = 4
QUAD = 4
VMEM_LIMIT = 32 * 1024 * 1024

f32 = jnp.float32
bf16 = jnp.bfloat16


def in_hbm(array):
    return pltpu.with_memory_space_constraint(array, pltpu.HBM)


def swap(block, mask, count):
    return lax.ppermute(block, "exp", [(i, i ^ mask) for i in range(count)])


def call(body, outs, ins, args, scratch=(), flops=0):
    moved = sum(a.size * a.dtype.itemsize for a in args)
    return pl.pallas_call(
        body,
        out_shape=outs,
        in_specs=ins,
        out_specs=jax.tree.map(lambda _: pl.BlockSpec(memory_space=pltpu.VMEM), outs),
        scratch_shapes=scratch,
        compiler_params=pltpu.CompilerParams(vmem_limit_bytes=VMEM_LIMIT),
        cost_estimate=pl.CostEstimate(flops=flops, bytes_accessed=moved, transcendentals=0),
    )(*args)


def weights_body(
    owner, taps, patch, prow, exposure, col_warp, row_warp,
    ring_ref, own_ref, first_ref, band, cols, rows_ref, select_ref, sums_ref,
    count_ref, blocks_ref,
    owner_ref, taps_ref, patch_ref, prow_ref, first_rows, last_rows, sems,
):
    height, width = exposure.shape
    nb = width // LANES
    count = owner_ref.shape[0]
    moves = [(taps, taps_ref), (owner, owner_ref), (patch, patch_ref), (prow, prow_ref)]
    small = [
        pltpu.make_async_copy(source, to, sems.at[4 + i]) for i, (source, to) in enumerate(moves)
    ]
    copies = [
        pltpu.make_async_copy(exposure.at[pl.ds(0, STRIP)], first_rows, sems.at[0]),
        pltpu.make_async_copy(exposure.at[pl.ds(height - STRIP, STRIP)], last_rows, sems.at[1]),
        pltpu.make_async_copy(col_warp, cols, sems.at[2]),
        pltpu.make_async_copy(row_warp, rows_ref, sems.at[3]),
    ]
    for copy in small + copies:
        copy.start()
    small[0].wait()

    delta = lax.broadcasted_iota(jnp.int32, (LANES, LANES), 0) - lax.broadcasted_iota(
        jnp.int32, (LANES, LANES), 1
    )
    tiles = {}
    for side in (-1, 0, 1):
        offset = delta + side * LANES + (TAPS - 1) // 2
        tile = jnp.zeros((LANES, LANES), f32)
        for tap in range(TAPS):
            tile = jnp.where(offset == tap, taps_ref[0:1, tap : tap + 1].astype(f32), tile)
        tiles[side] = tile.astype(bf16)
    for i in range(nb):
        for k in range(nb):
            tile = tiles.get(i - k, jnp.zeros((LANES, LANES), bf16))
            band[i * LANES : (i + 1) * LANES, k * LANES : (k + 1) * LANES] = tile

    for copy in small[1:]:
        copy.wait()
    me = lax.axis_index("exp")
    patch = patch_ref[...]
    slot = jnp.zeros_like(patch)
    for k in range(count):
        slot = jnp.where(patch == owner_ref[k], place_of(me ^ k, count), slot)
    key = slot * PATCH_ROWS + prow_ref[...]
    slots = lax.broadcasted_iota(jnp.int32, select_ref.shape, 0)
    select_ref[...] = jnp.where(slots == key, 1.0, 0.0).astype(bf16)

    ones = jnp.ones((select_ref.shape[1], LANES), bf16)
    held = jnp.dot(select_ref[...], ones, preferred_element_type=f32)
    lane = lax.broadcasted_iota(jnp.int32, (SUB, LANES), 1)
    for j in range(count):
        tile = jnp.zeros((SUB, LANES), f32)
        for s in range(PATCH_ROWS // SUB):
            at = j * PATCH_ROWS + s * SUB
            tile = jnp.where(lane == s, held[at : at + SUB], tile)
        count_ref[j * SUB : (j + 1) * SUB] = tile

    copies[0].wait()
    copies[1].wait()
    scale = 1.0 / (STRIP * LANES)
    for ref in (ring_ref, own_ref, first_ref):
        ref[...] = jnp.zeros_like(ref)
    for b in range(nb):
        at = slice(b * LANES, (b + 1) * LANES)
        means = []
        for ref in (first_rows, last_rows):
            column = jnp.sum(ref[:, at], axis=0, keepdims=True)
            total = jnp.sum(column, axis=1, keepdims=True)
            means.append(jnp.broadcast_to(total * scale, (1, LANES)))
        first, last = means
        own_ref[b : b + 1] = 0.5 * (first + last)
        first_ref[b : b + 1] = first
        ring_ref[b : b + 1] = last

    copies[2].wait()
    heads = {side: jnp.sum(tile.astype(f32), axis=0, keepdims=True) for side, tile in tiles.items()}
    blank = jnp.zeros((1, LANES), f32)
    lines = [
        jnp.concatenate([heads.get(b - k, blank) for k in range(nb)], axis=1) for b in range(nb)
    ]
    lines.append(jnp.zeros((own_ref.shape[0] - nb, width), f32))
    head = jnp.concatenate(lines, axis=0)
    upper = head.astype(bf16).astype(f32)
    stacked = jnp.concatenate([upper, head - upper], axis=0).astype(bf16)
    both = jnp.dot(stacked, cols[...], preferred_element_type=f32)
    total = both[: head.shape[0]] + both[head.shape[0] :]
    blocks_ref[...] = total
    base = own_ref.shape[0]
    for b in range(nb):
        for c in range(nb):
            to = base + b * nb + c
            ring_ref[to : to + 1] = total[b : b + 1, c * LANES : (c + 1) * LANES]

    copies[3].wait()
    ones = jnp.ones((row_warp.shape[1], LANES), bf16)
    rest = jnp.dot(rows_ref[...], ones, preferred_element_type=f32)
    total = jnp.zeros(sums_ref.shape, f32)
    for _ in range(2):
        part = rest.astype(bf16)
        rest = rest - part.astype(f32)
        total += jnp.dot(select_ref[...], part, preferred_element_type=f32)
    sums_ref[...] = total
    lane = lax.broadcasted_iota(jnp.int32, (PATCH_ROWS, LANES), 1)
    packed = jnp.zeros((PATCH_ROWS, LANES), f32)
    for j in range(count):
        packed = jnp.where(lane == j, total[j * PATCH_ROWS : (j + 1) * PATCH_ROWS], packed)
    ring_ref[ring_ref.shape[0] - PATCH_ROWS :] = packed


def local_body(own_ref, image, band, cols, rows, select, sums_ref, merged, warped):
    height, width = image.shape
    nb = width // LANES
    step = height // CHUNKS
    merged[...] = jnp.dot(band[...], cols[...], preferred_element_type=f32).astype(bf16)
    for i in range(CHUNKS):
        at = slice(i * step, (i + 1) * step)
        parts = []
        for b in range(nb):
            piece = image[at, b * LANES : (b + 1) * LANES] - own_ref[b : b + 1]
            parts.append(piece.astype(bf16))
        centred = jnp.concatenate(parts, axis=1)
        warped[at] = jnp.dot(centred, merged[...], preferred_element_type=f32).astype(bf16)
    values = jnp.dot(rows[...], warped[...], preferred_element_type=f32)
    high = values.astype(bf16)
    low = (values - high.astype(f32)).astype(bf16)
    sums_ref[...] = jnp.dot(select[...], high, preferred_element_type=f32) + jnp.dot(
        select[...], low, preferred_element_type=f32
    )


def place_of(mask, count):
    return (mask & 1) * (count // 2) + lax.shift_right_logical(mask, 1)


class Levels:
    def __init__(self, got_ref, first_ref, blocks_ref, rows_ref, count):
        nb = blocks_ref.shape[1] // LANES
        base = first_ref.shape[0]
        self.count, self.rows_ref = count, rows_ref
        self.packed = got_ref[got_ref.shape[0] - PATCH_ROWS :]
        self.lane = lax.broadcasted_iota(jnp.int32, (PATCH_ROWS, LANES), 1)
        self.own, self.other = [], []
        for c in range(nb):
            own = jnp.zeros((1, LANES), f32)
            other = jnp.zeros((1, LANES), f32)
            for b in range(nb):
                level = 0.5 * got_ref[b : b + 1]
                own += level * blocks_ref[b : b + 1, c * LANES : (c + 1) * LANES]
                at = base + b * nb + c
                other += 0.5 * first_ref[b : b + 1] * got_ref[at : at + 1]
            self.own.append(own)
            self.other.append(other)

    def terms(self, j):
        count = self.count
        me = lax.axis_index("exp")
        mask = (j % (count // 2)) * 2 + j // (count // 2)
        sender = lax.rem(me + count - 1, count)
        place = place_of(sender ^ me ^ mask, count)
        weight = self.rows_ref[j * PATCH_ROWS : (j + 1) * PATCH_ROWS]
        far = jnp.sum(jnp.where(self.lane == place, self.packed, 0.0), axis=1, keepdims=True)
        return [weight * own + far * other for own, other in zip(self.own, self.other)]


def send_body(got_ref, first_ref, blocks_ref, rows_ref, sums_ref, count_ref, out_ref):
    count = count_ref.shape[0] // SUB
    half = count // 2
    size = out_ref.shape[0] // half
    levels = Levels(got_ref, first_ref, blocks_ref, rows_ref, count)
    for j in range(half):
        at = (half + j) * PATCH_ROWS
        terms = levels.terms(half + j)
        for c, term in enumerate(terms):
            to = j * size + c * PATCH_ROWS
            part = sums_ref[at : at + PATCH_ROWS, c * LANES : (c + 1) * LANES]
            out_ref[to : to + PATCH_ROWS] = part + term
        to = j * size + len(terms) * PATCH_ROWS
        out_ref[to : to + SUB] = count_ref[(half + j) * SUB : (half + j + 1) * SUB]


def merge_body(
    got_ref, first_ref, blocks_ref, rows_ref, sums_ref, count_ref, half_ref, *out_refs
):
    count = count_ref.shape[0] // SUB
    half = count // 2
    size = half_ref.shape[0] // half
    levels = Levels(got_ref, first_ref, blocks_ref, rows_ref, count)
    for j in range(half):
        quad, far = j % QUAD, j // QUAD
        ref = out_refs[quad] if far == 0 else out_refs[QUAD + quad]
        base = 0 if far == 0 else (far - 1) * size
        at = j * PATCH_ROWS
        terms = levels.terms(j)
        for c, term in enumerate(terms):
            to = c * PATCH_ROWS
            part = sums_ref[at : at + PATCH_ROWS, c * LANES : (c + 1) * LANES]
            got = half_ref[j * size + to : j * size + to + PATCH_ROWS]
            ref[base + to : base + to + PATCH_ROWS] = part + term + got
        to = len(terms) * PATCH_ROWS
        got = half_ref[j * size + to : j * size + to + SUB]
        ref[base + to : base + to + SUB] = count_ref[j * SUB : (j + 1) * SUB] + got


def far_body(a_ref, b_ref, c_ref, d_ref, *out_refs):
    size = out_refs[0].shape[0]
    for i, ref in enumerate(out_refs):
        at = slice(i * size, (i + 1) * size)
        ref[...] = (a_ref[at] + b_ref[at]) + (c_ref[at] + d_ref[at])


def final_body(*refs):
    out_ref = refs[-1]
    total = refs[0][...]
    for ref in refs[1:-1]:
        total = total + ref[...]
    nb = out_ref.shape[1] // LANES
    held = total[nb * PATCH_ROWS :]
    for s in range(PATCH_ROWS // SUB):
        number = jnp.maximum(held[:, s : s + 1], 1.0)
        for c in range(nb):
            at = c * PATCH_ROWS + s * SUB
            out_ref[s * SUB : (s + 1) * SUB, c * LANES : (c + 1) * LANES] = (
                total[at : at + SUB] / number
            )


def on_device(exposure, psf_taps, col_warp, row_warp, row_patch, row_prow, owner_map):
    height, width = exposure.shape
    out_rows = row_warp.shape[0]
    count = lax.axis_size("exp")
    nb = width // LANES
    slots = count * PATCH_ROWS
    half, high_groups = count // 2, count // (2 * QUAD)
    size = PATCH_ROWS * nb + SUB
    vmem = pl.BlockSpec(memory_space=pltpu.VMEM)
    hbm = pl.BlockSpec(memory_space=pltpu.HBM)

    def shape(*dims):
        return jax.ShapeDtypeStruct(dims, f32)

    tile = shape(-(-nb // SUB) * SUB, LANES)
    ring, own, first, band, cols, rows, select, weights, held, blocks = call(
        weights_body,
        [shape(tile.shape[0] + nb * nb + PATCH_ROWS, LANES), tile, tile,
         jax.ShapeDtypeStruct((width, width), bf16), jax.ShapeDtypeStruct(col_warp.shape, bf16),
         jax.ShapeDtypeStruct(row_warp.shape, bf16),
         jax.ShapeDtypeStruct((slots, out_rows), bf16), shape(slots, LANES),
         shape(count * SUB, LANES), shape(tile.shape[0], width)],
        [hbm] * 7,
        tuple(in_hbm(array) for array in (
            owner_map, psf_taps, row_patch.reshape(1, out_rows), row_prow.reshape(1, out_rows),
            exposure, col_warp, row_warp,
        )),
        scratch=[
            pltpu.SMEM(owner_map.shape, jnp.int32),
            pltpu.VMEM(psf_taps.shape, bf16),
            pltpu.VMEM((1, out_rows), jnp.int32),
            pltpu.VMEM((1, out_rows), jnp.int32),
            pltpu.VMEM((STRIP, width), f32),
            pltpu.VMEM((STRIP, width), f32),
            pltpu.SemaphoreType.DMA((8,)),
        ],
        flops=2 * width * width * width,
    )
    ring = lax.ppermute(ring, "exp", [(i, (i + 1) % count) for i in range(count)])
    sums = call(
        local_body, shape(slots, width), [vmem] * 6,
        (own, exposure, band, cols, rows, select),
        scratch=[pltpu.VMEM((width, width), bf16), pltpu.VMEM((height, width), bf16)],
        flops=2 * height * width * (width + out_rows) + 4 * slots * out_rows * width,
    )
    common = (ring, first, blocks, weights, sums, held)
    send = call(send_body, shape(half * size, LANES), [vmem] * 6, common)
    got = swap(send, 1, count)

    shapes = [shape(size, LANES)] * QUAD
    if high_groups > 1:
        shapes += [shape((high_groups - 1) * size, LANES)] * QUAD
    parts = call(merge_body, shapes, [vmem] * 7, common + (got,))
    near, far = parts[:QUAD], parts[QUAD:]
    terms = [near[0]]
    if high_groups > 1:
        far = [far[0]] + [swap(far[q], 2 * q, count) for q in range(QUAD - 1, 0, -1)]
    near_got = [swap(near[q], 2 * q, count) for q in range(QUAD - 1, 0, -1)]
    if high_groups > 1:
        sent = call(far_body, [shape(size, LANES)] * (high_groups - 1), [vmem] * QUAD, far)
        terms += [swap(sent[h - 1], 2 * QUAD * h, count) for h in range(1, high_groups)]
    terms += near_got
    return call(final_body, shape(PATCH_ROWS, width), [vmem] * len(terms), tuple(terms))


def solution(mesh):
    placed = (
        P(("band", "exp"), None),
        P(("band", "exp"), None),
        P(("band", "exp"), None),
        P(("band", "exp"), None),
        P(("band", "exp"), None),
        P(("band", "exp")),
        P("band"),
    )
    return jax.shard_map(
        on_device, mesh=mesh, in_specs=placed, out_specs=P(("band", "exp"), None), check_vma=False
    )
```

```python
import jax
import jax.numpy as jnp
from jax import lax
from jax.experimental import pallas as pl
from jax.experimental.pallas import tpu as pltpu
from jax.sharding import PartitionSpec as P

STRIP = 16
TAPS = 15
PATCH_ROWS = 32
LANES = 128
SUB = 8
CHUNKS = 4
QUAD = 4
VMEM_LIMIT = 32 * 1024 * 1024

f32 = jnp.float32
bf16 = jnp.bfloat16


def in_hbm(array):
    return pltpu.with_memory_space_constraint(array, pltpu.HBM)


def swap(block, mask, count):
    return lax.ppermute(block, "exp", [(i, i ^ mask) for i in range(count)])


def call(body, outs, ins, args, scratch=(), flops=0):
    moved = sum(a.size * a.dtype.itemsize for a in args)
    return pl.pallas_call(
        body,
        out_shape=outs,
        in_specs=ins,
        out_specs=jax.tree.map(lambda _: pl.BlockSpec(memory_space=pltpu.VMEM), outs),
        scratch_shapes=scratch,
        compiler_params=pltpu.CompilerParams(vmem_limit_bytes=VMEM_LIMIT),
        cost_estimate=pl.CostEstimate(flops=flops, bytes_accessed=moved, transcendentals=0),
    )(*args)


def lane_dot(left, right):
    return lax.dot_general(left, right, (((1,), (1,)), ((), ())), preferred_element_type=f32)


def parts_of(values):
    high = values.astype(bf16)
    return high, (values - high.astype(f32)).astype(bf16)


def band_tiles(taps):
    half = (TAPS - 1) // 2
    delta = lax.broadcasted_iota(jnp.int32, (LANES, LANES), 0) - lax.broadcasted_iota(
        jnp.int32, (LANES, LANES), 1
    )
    middle = jnp.zeros((LANES, LANES), f32)
    upper = jnp.zeros((SUB, LANES), f32)
    lower = jnp.zeros((SUB, LANES), f32)
    for tap in range(TAPS):
        value = jnp.broadcast_to(taps[:, tap : tap + 1], (1, LANES))
        middle = jnp.where(delta == tap - half, value, middle)
        if tap > half:
            upper = jnp.where(delta[:SUB] == tap - half - LANES, value, upper)
        if tap < half:
            lower = jnp.where(delta[LANES - SUB :] == tap - half + LANES, value, lower)
    rest = jnp.zeros((LANES - SUB, LANES), f32)
    return {
        0: middle,
        -1: jnp.concatenate([rest, lower], axis=0),
        1: jnp.concatenate([upper, rest], axis=0),
    }


def weights_body(
    owner, taps, patch, prow, exposure, col_warp, row_warp,
    ring_ref, own_ref, first_ref, merged_ref, rows_ref, select_ref, lines_ref, blocks_ref,
    owner_ref, taps_ref, patch_ref, prow_ref, first_rows, last_rows, cols, band, sems,
):
    height, width = exposure.shape
    nb = width // LANES
    count = owner_ref.shape[0]
    moves = [
        (taps, taps_ref), (owner, owner_ref), (patch, patch_ref), (prow, prow_ref),
        (col_warp, cols),
        (exposure.at[pl.ds(0, STRIP)], first_rows),
        (exposure.at[pl.ds(height - STRIP, STRIP)], last_rows),
        (row_warp, rows_ref),
    ]
    copies = [pltpu.make_async_copy(*move, sems.at[i]) for i, move in enumerate(moves)]
    for copy in copies:
        copy.start()

    copies[0].wait()
    tiles = band_tiles(taps_ref[...].astype(f32))
    tiles = {side: tile.astype(bf16) for side, tile in tiles.items()}
    for i in range(nb):
        for k in range(nb):
            tile = tiles.get(k - i, jnp.zeros((LANES, LANES), bf16))
            band[k * LANES : (k + 1) * LANES, i * LANES : (i + 1) * LANES] = tile

    for copy in copies[1:4]:
        copy.wait()
    me = lax.axis_index("exp")
    patch = patch_ref[...]
    slot = jnp.zeros_like(patch)
    for k in range(count):
        slot = jnp.where(patch == owner_ref[k], place_of(me ^ k, count), slot)
    key = slot * PATCH_ROWS + prow_ref[...]
    slots = lax.broadcasted_iota(jnp.int32, select_ref.shape, 0)
    select_ref[...] = jnp.where(slots == key, 1.0, 0.0).astype(bf16)

    copies[4].wait()
    both = jnp.dot(band[...], cols[...], preferred_element_type=f32)
    merged_ref[...] = both.astype(bf16)
    for ref in (ring_ref, own_ref, first_ref, blocks_ref, lines_ref):
        ref[...] = jnp.zeros_like(ref)
    base = own_ref.shape[0]
    for b in range(nb):
        total = jnp.sum(both[b * LANES : (b + 1) * LANES], axis=0, keepdims=True)
        blocks_ref[b : b + 1] = total
        for c in range(nb):
            to = base + b * nb + c
            ring_ref[to : to + 1] = total[:, c * LANES : (c + 1) * LANES]

    copies[5].wait()
    copies[6].wait()
    scale = 1.0 / (STRIP * LANES)
    for b in range(nb):
        at = slice(b * LANES, (b + 1) * LANES)
        means = []
        for ref in (first_rows, last_rows):
            column = jnp.sum(ref[:, at], axis=0, keepdims=True)
            total = jnp.sum(column, axis=1, keepdims=True)
            means.append(jnp.broadcast_to(total * scale, (1, LANES)))
        first, last = means
        own_ref[b : b + 1] = 0.5 * (first + last)
        first_ref[b : b + 1] = first
        ring_ref[b : b + 1] = last

    copies[7].wait()
    partial = rows_ref[:, :LANES].astype(f32)
    for i in range(1, height // LANES):
        partial += rows_ref[:, i * LANES : (i + 1) * LANES].astype(f32)
    ones = jnp.ones((2 * SUB, LANES), bf16)
    high, low = parts_of(partial)
    high, low = parts_of(lane_dot(ones, high) + lane_dot(ones, low))
    line = lax.broadcasted_iota(jnp.int32, high.shape, 0)
    left = jnp.where(line == 0, high.astype(f32), jnp.where(line == 1, low.astype(f32), 1.0))
    found = lane_dot(left.astype(bf16), select_ref[...])
    weight = found[0:1] + found[1:2]
    lines_ref[0:1] = weight
    lines_ref[1:2] = found[2:3]
    base += nb * nb
    for i in range(weight.shape[1] // LANES):
        ring_ref[base + i : base + i + 1] = weight[:, i * LANES : (i + 1) * LANES]


def local_body(own_ref, image, merged, rows, select, sums_ref, warped):
    height, width = image.shape
    nb = width // LANES
    step = height // CHUNKS
    for i in range(CHUNKS):
        at = slice(i * step, (i + 1) * step)
        parts = []
        for b in range(nb):
            piece = image[at, b * LANES : (b + 1) * LANES] - own_ref[b : b + 1]
            parts.append(piece.astype(bf16))
        centred = jnp.concatenate(parts, axis=1)
        warped[at] = jnp.dot(centred, merged[...], preferred_element_type=f32).astype(bf16)
    values = jnp.dot(rows[...], warped[...], preferred_element_type=f32)
    high, low = parts_of(values)
    sums_ref[...] = jnp.dot(select[...], high, preferred_element_type=f32) + jnp.dot(
        select[...], low, preferred_element_type=f32
    )


def place_of(mask, count):
    return (mask & 1) * (count // 2) + lax.shift_right_logical(mask, 1)


def upright(line, start):
    shape = (PATCH_ROWS, LANES)
    wanted = lax.broadcasted_iota(jnp.int32, shape, 1) == start + lax.broadcasted_iota(
        jnp.int32, shape, 0
    )
    return jnp.sum(jnp.where(wanted, line, 0.0), axis=1, keepdims=True)


class Levels:
    def __init__(self, got_ref, first_ref, blocks_ref, lines_ref, count):
        nb = blocks_ref.shape[1] // LANES
        base = first_ref.shape[0]
        self.count, self.lines_ref, self.got_ref = count, lines_ref, got_ref
        self.base = base + nb * nb
        self.own, self.other = [], []
        for c in range(nb):
            own = jnp.zeros((1, LANES), f32)
            other = jnp.zeros((1, LANES), f32)
            for b in range(nb):
                level = 0.5 * got_ref[b : b + 1]
                own += level * blocks_ref[b : b + 1, c * LANES : (c + 1) * LANES]
                at = base + b * nb + c
                other += 0.5 * first_ref[b : b + 1] * got_ref[at : at + 1]
            self.own.append(own)
            self.other.append(other)

    def terms(self, j):
        count, each = self.count, LANES // PATCH_ROWS
        me = lax.axis_index("exp")
        mask = (j % (count // 2)) * 2 + j // (count // 2)
        sender = lax.rem(me + count - 1, count)
        place = place_of(sender ^ me ^ mask, count)
        at = j // each * LANES
        weight = upright(self.lines_ref[0:1, at : at + LANES], j % each * PATCH_ROWS)
        line = self.got_ref[pl.ds(self.base + place // each, 1)]
        far = upright(line, lax.rem(place, each) * PATCH_ROWS)
        return [weight * own + far * other for own, other in zip(self.own, self.other)]

    def held(self, j):
        each = LANES // PATCH_ROWS
        at = j // each * LANES
        line = jnp.broadcast_to(self.lines_ref[1:2, at : at + LANES], (SUB, LANES))
        start = j % each * PATCH_ROWS
        return pltpu.roll(line, LANES - start, 1) if start else line


def send_body(got_ref, first_ref, blocks_ref, lines_ref, sums_ref, out_ref):
    count = sums_ref.shape[0] // PATCH_ROWS
    half = count // 2
    size = out_ref.shape[0] // half
    levels = Levels(got_ref, first_ref, blocks_ref, lines_ref, count)
    for j in range(half):
        at = (half + j) * PATCH_ROWS
        terms = levels.terms(half + j)
        for c, term in enumerate(terms):
            to = j * size + c * PATCH_ROWS
            part = sums_ref[at : at + PATCH_ROWS, c * LANES : (c + 1) * LANES]
            out_ref[to : to + PATCH_ROWS] = part + term
        to = j * size + len(terms) * PATCH_ROWS
        out_ref[to : to + SUB] = levels.held(half + j)


def merge_body(got_ref, first_ref, blocks_ref, lines_ref, sums_ref, half_ref, *out_refs):
    count = sums_ref.shape[0] // PATCH_ROWS
    half = count // 2
    size = half_ref.shape[0] // half
    levels = Levels(got_ref, first_ref, blocks_ref, lines_ref, count)
    for j in range(half):
        quad, far = j % QUAD, j // QUAD
        ref = out_refs[quad] if far == 0 else out_refs[QUAD + quad]
        base = 0 if far == 0 else (far - 1) * size
        at = j * PATCH_ROWS
        terms = levels.terms(j)
        for c, term in enumerate(terms):
            to = c * PATCH_ROWS
            part = sums_ref[at : at + PATCH_ROWS, c * LANES : (c + 1) * LANES]
            got = half_ref[j * size + to : j * size + to + PATCH_ROWS]
            ref[base + to : base + to + PATCH_ROWS] = part + term + got
        to = len(terms) * PATCH_ROWS
        got = half_ref[j * size + to : j * size + to + SUB]
        ref[base + to : base + to + SUB] = levels.held(j) + got


def far_body(a_ref, b_ref, c_ref, d_ref, *out_refs):
    size = out_refs[0].shape[0]
    for i, ref in enumerate(out_refs):
        at = slice(i * size, (i + 1) * size)
        ref[...] = (a_ref[at] + b_ref[at]) + (c_ref[at] + d_ref[at])


def final_body(*refs):
    out_ref = refs[-1]
    total = refs[0][...]
    for ref in refs[1:-1]:
        total = total + ref[...]
    nb = out_ref.shape[1] // LANES
    number = jnp.maximum(upright(total[nb * PATCH_ROWS : nb * PATCH_ROWS + 1], 0), 1.0)
    for c in range(nb):
        part = total[c * PATCH_ROWS : (c + 1) * PATCH_ROWS]
        out_ref[:, c * LANES : (c + 1) * LANES] = part / number


def on_device(exposure, psf_taps, col_warp, row_warp, row_patch, row_prow, owner_map):
    height, width = exposure.shape
    out_rows = row_warp.shape[0]
    count = lax.axis_size("exp")
    nb = width // LANES
    slots = count * PATCH_ROWS
    half, high_groups = count // 2, count // (2 * QUAD)
    size = PATCH_ROWS * nb + SUB
    vmem = pl.BlockSpec(memory_space=pltpu.VMEM)
    hbm = pl.BlockSpec(memory_space=pltpu.HBM)

    def shape(*dims):
        return jax.ShapeDtypeStruct(dims, f32)

    tile = shape(-(-nb // SUB) * SUB, LANES)
    ring_rows = tile.shape[0] + nb * nb + slots // LANES
    ring, own, first, merged, rows, select, lines, blocks = call(
        weights_body,
        [shape(-(-ring_rows // SUB) * SUB, LANES), tile, tile,
         jax.ShapeDtypeStruct((width, width), bf16), jax.ShapeDtypeStruct(row_warp.shape, bf16),
         jax.ShapeDtypeStruct((slots, out_rows), bf16), shape(SUB, slots),
         shape(tile.shape[0], width)],
        [hbm] * 7,
        tuple(in_hbm(array) for array in (
            owner_map, psf_taps, row_patch.reshape(1, out_rows), row_prow.reshape(1, out_rows),
            exposure, col_warp, row_warp,
        )),
        scratch=[
            pltpu.SMEM(owner_map.shape, jnp.int32),
            pltpu.VMEM(psf_taps.shape, bf16),
            pltpu.VMEM((1, out_rows), jnp.int32),
            pltpu.VMEM((1, out_rows), jnp.int32),
            pltpu.VMEM((STRIP, width), f32),
            pltpu.VMEM((STRIP, width), f32),
            pltpu.VMEM(col_warp.shape, bf16),
            pltpu.VMEM((width, width), bf16),
            pltpu.SemaphoreType.DMA((8,)),
        ],
        flops=2 * width * width * width,
    )
    ring = lax.ppermute(ring, "exp", [(i, (i + 1) % count) for i in range(count)])
    sums = call(
        local_body, shape(slots, width), [vmem] * 5, (own, exposure, merged, rows, select),
        scratch=[pltpu.VMEM((height, width), bf16)],
        flops=2 * height * width * (width + out_rows) + 4 * slots * out_rows * width,
    )
    common = (ring, first, blocks, lines, sums)
    send = call(send_body, shape(half * size, LANES), [vmem] * 5, common)
    got = swap(send, 1, count)

    shapes = [shape(size, LANES)] * QUAD
    if high_groups > 1:
        shapes += [shape((high_groups - 1) * size, LANES)] * QUAD
    parts = call(merge_body, shapes, [vmem] * 6, common + (got,))
    near, far = parts[:QUAD], parts[QUAD:]
    terms = [near[0]]
    if high_groups > 1:
        far = [far[0]] + [swap(far[q], 2 * q, count) for q in range(QUAD - 1, 0, -1)]
    near_got = [swap(near[q], 2 * q, count) for q in range(QUAD - 1, 0, -1)]
    if high_groups > 1:
        sent = call(far_body, [shape(size, LANES)] * (high_groups - 1), [vmem] * QUAD, far)
        terms += [swap(sent[h - 1], 2 * QUAD * h, count) for h in range(1, high_groups)]
    terms += near_got
    return call(final_body, shape(PATCH_ROWS, width), [vmem] * len(terms), tuple(terms))


def solution(mesh):
    placed = (
        P(("band", "exp"), None),
        P(("band", "exp"), None),
        P(("band", "exp"), None),
        P(("band", "exp"), None),
        P(("band", "exp"), None),
        P(("band", "exp")),
        P("band"),
    )
    return jax.shard_map(
        on_device, mesh=mesh, in_specs=placed, out_specs=P(("band", "exp"), None), check_vma=False
    )
```

```python
import functools

import jax
import jax.numpy as jnp
from jax import lax
from jax.experimental import pallas as pl
from jax.experimental.pallas import tpu as pltpu
from jax.sharding import PartitionSpec as P

STRIP = 16
TAPS = 15
PATCH_ROWS = 32
LANES = 128
SUB = 8
CHUNKS = 4
QUAD = 4
FAR_ORDER = (2, 1, 3)
NEAR_ORDER = (3, 2, 1)
VMEM_LIMIT = 32 * 1024 * 1024

f32 = jnp.float32
bf16 = jnp.bfloat16


def in_hbm(array):
    return pltpu.with_memory_space_constraint(array, pltpu.HBM)


def swap(block, mask, count):
    return lax.ppermute(block, "exp", [(i, i ^ mask) for i in range(count)])


def call(body, outs, ins, args, scratch=(), flops=0):
    moved = sum(a.size * a.dtype.itemsize for a in args)
    return pl.pallas_call(
        body,
        out_shape=outs,
        in_specs=ins,
        out_specs=jax.tree.map(lambda _: pl.BlockSpec(memory_space=pltpu.VMEM), outs),
        scratch_shapes=scratch,
        compiler_params=pltpu.CompilerParams(vmem_limit_bytes=VMEM_LIMIT),
        cost_estimate=pl.CostEstimate(flops=flops, bytes_accessed=moved, transcendentals=0),
    )(*args)


def lane_dot(left, right):
    return lax.dot_general(left, right, (((1,), (1,)), ((), ())), preferred_element_type=f32)


def parts_of(values):
    high = values.astype(bf16)
    return high, (values - high.astype(f32)).astype(bf16)


def band_tiles(taps):
    half = (TAPS - 1) // 2
    delta = lax.broadcasted_iota(jnp.int32, (LANES, LANES), 0) - lax.broadcasted_iota(
        jnp.int32, (LANES, LANES), 1
    )
    middle = jnp.zeros((LANES, LANES), f32)
    upper = jnp.zeros((SUB, LANES), f32)
    lower = jnp.zeros((SUB, LANES), f32)
    for tap in range(TAPS):
        value = jnp.broadcast_to(taps[:, tap : tap + 1], (1, LANES))
        middle = jnp.where(delta == tap - half, value, middle)
        if tap > half:
            upper = jnp.where(delta[:SUB] == tap - half - LANES, value, upper)
        if tap < half:
            lower = jnp.where(delta[LANES - SUB :] == tap - half + LANES, value, lower)
    rest = jnp.zeros((LANES - SUB, LANES), f32)
    return {
        0: middle,
        -1: jnp.concatenate([rest, lower], axis=0),
        1: jnp.concatenate([upper, rest], axis=0),
    }


def weights_body(
    owner, taps, patch, prow, exposure, col_warp, row_warp,
    ring_ref, own_ref, first_ref, merged_ref, rows_ref, select_ref, lines_ref, blocks_ref,
    owner_ref, taps_ref, patch_ref, prow_ref, first_rows, last_rows, cols, band, sems,
):
    height, width = exposure.shape
    nb = width // LANES
    count = owner_ref.shape[0]
    moves = [
        (taps, taps_ref), (owner, owner_ref), (patch, patch_ref), (prow, prow_ref),
        (col_warp, cols),
        (exposure.at[pl.ds(0, STRIP)], first_rows),
        (exposure.at[pl.ds(height - STRIP, STRIP)], last_rows),
        (row_warp, rows_ref),
    ]
    copies = [pltpu.make_async_copy(*move, sems.at[i]) for i, move in enumerate(moves)]
    for copy in copies:
        copy.start()

    copies[0].wait()
    tiles = band_tiles(taps_ref[...].astype(f32))
    tiles = {side: tile.astype(bf16) for side, tile in tiles.items()}
    for i in range(nb):
        for k in range(nb):
            tile = tiles.get(k - i, jnp.zeros((LANES, LANES), bf16))
            band[k * LANES : (k + 1) * LANES, i * LANES : (i + 1) * LANES] = tile

    for copy in copies[1:4]:
        copy.wait()
    me = lax.axis_index("exp")
    patch = patch_ref[...]
    slot = jnp.zeros_like(patch)
    for k in range(count):
        slot = jnp.where(patch == owner_ref[k], place_of(me ^ k, count), slot)
    key = slot * PATCH_ROWS + prow_ref[...]
    slots = lax.broadcasted_iota(jnp.int32, select_ref.shape, 0)
    select_ref[...] = jnp.where(slots == key, 1.0, 0.0).astype(bf16)

    copies[4].wait()
    both = jnp.dot(band[...], cols[...], preferred_element_type=f32)
    merged_ref[...] = both.astype(bf16)
    for ref in (ring_ref, own_ref, first_ref, blocks_ref, lines_ref):
        ref[...] = jnp.zeros_like(ref)
    base = own_ref.shape[0]
    for b in range(nb):
        total = jnp.sum(both[b * LANES : (b + 1) * LANES], axis=0, keepdims=True)
        blocks_ref[b : b + 1] = total
        for c in range(nb):
            to = base + b * nb + c
            ring_ref[to : to + 1] = total[:, c * LANES : (c + 1) * LANES]

    copies[5].wait()
    copies[6].wait()
    scale = 1.0 / (STRIP * LANES)
    for b in range(nb):
        at = slice(b * LANES, (b + 1) * LANES)
        means = []
        for ref in (first_rows, last_rows):
            column = jnp.sum(ref[:, at], axis=0, keepdims=True)
            total = jnp.sum(column, axis=1, keepdims=True)
            means.append(jnp.broadcast_to(total * scale, (1, LANES)))
        first, last = means
        own_ref[b : b + 1] = 0.5 * (first + last)
        first_ref[b : b + 1] = first
        ring_ref[b : b + 1] = last

    copies[7].wait()
    partial = rows_ref[:, :LANES].astype(f32)
    for i in range(1, height // LANES):
        partial += rows_ref[:, i * LANES : (i + 1) * LANES].astype(f32)
    ones = jnp.ones((2 * SUB, LANES), bf16)
    high, low = parts_of(partial)
    high, low = parts_of(lane_dot(ones, high) + lane_dot(ones, low))
    line = lax.broadcasted_iota(jnp.int32, high.shape, 0)
    left = jnp.where(line == 0, high.astype(f32), jnp.where(line == 1, low.astype(f32), 1.0))
    found = lane_dot(left.astype(bf16), select_ref[...])
    weight = found[0:1] + found[1:2]
    lines_ref[0:1] = weight
    lines_ref[1:2] = found[2:3]
    base += nb * nb
    for i in range(weight.shape[1] // LANES):
        ring_ref[base + i : base + i + 1] = weight[:, i * LANES : (i + 1) * LANES]


def local_body(own_ref, image, merged, rows, select, sums_ref, high_ref, low_ref, warped):
    height, width = image.shape
    nb = width // LANES
    step = height // CHUNKS
    for i in range(CHUNKS):
        at = slice(i * step, (i + 1) * step)
        parts = []
        for b in range(nb):
            piece = image[at, b * LANES : (b + 1) * LANES] - own_ref[b : b + 1]
            parts.append(piece.astype(bf16))
        centred = jnp.concatenate(parts, axis=1)
        warped[at] = jnp.dot(centred, merged[...], preferred_element_type=f32).astype(bf16)
    high, low = parts_of(jnp.dot(rows[...], warped[...], preferred_element_type=f32))
    high_ref[...] = high
    low_ref[...] = low
    far = select[: sums_ref.shape[0]]
    sums_ref[...] = jnp.dot(far, high, preferred_element_type=f32) + jnp.dot(
        far, low, preferred_element_type=f32
    )


def place_of(mask, count):
    other, at = mask & 1, lax.shift_right_logical(mask, 1)
    far = count // 2 - QUAD
    return jnp.where(at < QUAD, 2 * far + other * QUAD + at, other * far + at - QUAD)


def mask_of(place, count):
    far = count // 2 - QUAD
    if place < 2 * far:
        return (place % far + QUAD) * 2 + place // far
    return (place - 2 * far) % QUAD * 2 + (place - 2 * far) // QUAD


def upright(line, start):
    shape = (PATCH_ROWS, LANES)
    wanted = lax.broadcasted_iota(jnp.int32, shape, 1) == start + lax.broadcasted_iota(
        jnp.int32, shape, 0
    )
    return jnp.sum(jnp.where(wanted, line, 0.0), axis=1, keepdims=True)


class Levels:
    def __init__(self, got_ref, first_ref, blocks_ref, lines_ref, count):
        nb = blocks_ref.shape[1] // LANES
        base = first_ref.shape[0]
        self.count, self.lines_ref, self.got_ref = count, lines_ref, got_ref
        self.base = base + nb * nb
        self.own, self.other = [], []
        for c in range(nb):
            own = jnp.zeros((1, LANES), f32)
            other = jnp.zeros((1, LANES), f32)
            for b in range(nb):
                level = 0.5 * got_ref[b : b + 1]
                own += level * blocks_ref[b : b + 1, c * LANES : (c + 1) * LANES]
                at = base + b * nb + c
                other += 0.5 * first_ref[b : b + 1] * got_ref[at : at + 1]
            self.own.append(own)
            self.other.append(other)

    def terms(self, j):
        count, each = self.count, LANES // PATCH_ROWS
        me = lax.axis_index("exp")
        mask = mask_of(j, count)
        sender = lax.rem(me + count - 1, count)
        place = place_of(sender ^ me ^ mask, count)
        at = j // each * LANES
        weight = upright(self.lines_ref[0:1, at : at + LANES], j % each * PATCH_ROWS)
        line = self.got_ref[pl.ds(self.base + place // each, 1)]
        far = upright(line, lax.rem(place, each) * PATCH_ROWS)
        return [weight * own + far * other for own, other in zip(self.own, self.other)]

    def held(self, j):
        each = LANES // PATCH_ROWS
        at = j // each * LANES
        line = jnp.broadcast_to(self.lines_ref[1:2, at : at + LANES], (SUB, LANES))
        start = j % each * PATCH_ROWS
        return pltpu.roll(line, LANES - start, 1) if start else line


def put_block(ref, at, size, sums, levels, place, got=None):
    terms = levels.terms(place)
    for c, term in enumerate(terms):
        to = slice(at * size + c * PATCH_ROWS, at * size + (c + 1) * PATCH_ROWS)
        value = sums[:, c * LANES : (c + 1) * LANES] + term
        ref[to] = value if got is None else value + got[c * PATCH_ROWS : (c + 1) * PATCH_ROWS]
    to = at * size + len(terms) * PATCH_ROWS
    held = levels.held(place)
    ref[to : to + SUB] = held if got is None else held + got[size - SUB :]


def far_send_body(count, got_ref, first_ref, blocks_ref, lines_ref, sums_ref, out_ref):
    far = count // 2 - QUAD
    size = out_ref.shape[0] // far
    levels = Levels(got_ref, first_ref, blocks_ref, lines_ref, count)
    for j in range(far):
        at = (far + j) * PATCH_ROWS
        put_block(out_ref, j, size, sums_ref[at : at + PATCH_ROWS], levels, far + j)


def near_body(
    count, got_ref, first_ref, blocks_ref, lines_ref, select, high, low, send_ref, keep_ref
):
    far = count // 2 - QUAD
    size = send_ref.shape[0] // QUAD
    levels = Levels(got_ref, first_ref, blocks_ref, lines_ref, count)
    near = select[2 * far * PATCH_ROWS :]
    sums = jnp.dot(near, high[...], preferred_element_type=f32) + jnp.dot(
        near, low[...], preferred_element_type=f32
    )
    for part, ref in enumerate((keep_ref, send_ref)):
        for j in range(QUAD):
            at = (part * QUAD + j) * PATCH_ROWS
            place = 2 * far + part * QUAD + j
            put_block(ref, j, size, sums[at : at + PATCH_ROWS], levels, place)


def far_merge_body(
    count, got_ref, first_ref, blocks_ref, lines_ref, sums_ref, half_ref, *out_refs
):
    far = count // 2 - QUAD
    size = half_ref.shape[0] // far
    levels = Levels(got_ref, first_ref, blocks_ref, lines_ref, count)
    for j in range(far):
        at = j * PATCH_ROWS
        got = half_ref[j * size : (j + 1) * size]
        put_block(
            out_refs[j % QUAD], j // QUAD, size, sums_ref[at : at + PATCH_ROWS], levels, j, got
        )


def near_merge_body(keep_ref, got_ref, *out_refs):
    size = out_refs[0].shape[0]
    for j, ref in enumerate(out_refs):
        at = slice(j * size, (j + 1) * size)
        ref[...] = keep_ref[at] + got_ref[at]


def far_body(a_ref, b_ref, c_ref, d_ref, *out_refs):
    size = out_refs[0].shape[0]
    for i, ref in enumerate(out_refs):
        at = slice(i * size, (i + 1) * size)
        ref[...] = (a_ref[at] + b_ref[at]) + (c_ref[at] + d_ref[at])


def final_body(*refs):
    out_ref = refs[-1]
    total = refs[0][...]
    for ref in refs[1:-1]:
        total = total + ref[...]
    nb = out_ref.shape[1] // LANES
    number = jnp.maximum(upright(total[nb * PATCH_ROWS : nb * PATCH_ROWS + 1], 0), 1.0)
    for c in range(nb):
        part = total[c * PATCH_ROWS : (c + 1) * PATCH_ROWS]
        out_ref[:, c * LANES : (c + 1) * LANES] = part / number


def on_device(exposure, psf_taps, col_warp, row_warp, row_patch, row_prow, owner_map):
    height, width = exposure.shape
    out_rows = row_warp.shape[0]
    count = lax.axis_size("exp")
    nb = width // LANES
    slots = count * PATCH_ROWS
    half, high_groups = count // 2, count // (2 * QUAD)
    size = PATCH_ROWS * nb + SUB
    vmem = pl.BlockSpec(memory_space=pltpu.VMEM)
    hbm = pl.BlockSpec(memory_space=pltpu.HBM)

    def shape(*dims):
        return jax.ShapeDtypeStruct(dims, f32)

    tile = shape(-(-nb // SUB) * SUB, LANES)
    ring_rows = tile.shape[0] + nb * nb + slots // LANES
    ring, own, first, merged, rows, select, lines, blocks = call(
        weights_body,
        [shape(-(-ring_rows // SUB) * SUB, LANES), tile, tile,
         jax.ShapeDtypeStruct((width, width), bf16), jax.ShapeDtypeStruct(row_warp.shape, bf16),
         jax.ShapeDtypeStruct((slots, out_rows), bf16), shape(SUB, slots),
         shape(tile.shape[0], width)],
        [hbm] * 7,
        tuple(in_hbm(array) for array in (
            owner_map, psf_taps, row_patch.reshape(1, out_rows), row_prow.reshape(1, out_rows),
            exposure, col_warp, row_warp,
        )),
        scratch=[
            pltpu.SMEM(owner_map.shape, jnp.int32),
            pltpu.VMEM(psf_taps.shape, bf16),
            pltpu.VMEM((1, out_rows), jnp.int32),
            pltpu.VMEM((1, out_rows), jnp.int32),
            pltpu.VMEM((STRIP, width), f32),
            pltpu.VMEM((STRIP, width), f32),
            pltpu.VMEM(col_warp.shape, bf16),
            pltpu.VMEM((width, width), bf16),
            pltpu.SemaphoreType.DMA((8,)),
        ],
        flops=2 * width * width * width,
    )
    ring = lax.ppermute(ring, "exp", [(i, (i + 1) % count) for i in range(count)])
    far = half - QUAD
    sums, high, low = call(
        local_body,
        [shape(2 * far * PATCH_ROWS, width)] + [jax.ShapeDtypeStruct((out_rows, width), bf16)] * 2,
        [vmem] * 5, (own, exposure, merged, rows, select),
        scratch=[pltpu.VMEM((height, width), bf16)],
        flops=2 * height * width * (width + out_rows) + 4 * slots * out_rows * width,
    )
    common = (ring, first, blocks, lines)
    far_send = call(
        functools.partial(far_send_body, count), shape(far * size, LANES), [vmem] * 5,
        common + (sums,),
    )
    far_got = swap(far_send, 1, count)
    near_send, near_keep = call(
        functools.partial(near_body, count), [shape(QUAD * size, LANES)] * 2, [vmem] * 7,
        common + (select, high, low),
    )
    near_got = swap(near_send, 1, count)
    parts = call(
        functools.partial(far_merge_body, count),
        [shape((high_groups - 1) * size, LANES)] * QUAD, [vmem] * 6, common + (sums, far_got),
    )
    terms = [parts[0]] + [swap(parts[q], 2 * q, count) for q in FAR_ORDER]
    near = call(near_merge_body, [shape(size, LANES)] * QUAD, [vmem] * 2, (near_keep, near_got))
    rest = [near[0]] + [swap(near[q], 2 * q, count) for q in NEAR_ORDER]
    sent = call(far_body, [shape(size, LANES)] * (high_groups - 1), [vmem] * QUAD, terms)
    rest = [swap(sent[h - 1], 2 * QUAD * h, count) for h in range(1, high_groups)] + rest
    return call(final_body, shape(PATCH_ROWS, width), [vmem] * len(rest), tuple(rest))


def solution(mesh):
    placed = (
        P(("band", "exp"), None),
        P(("band", "exp"), None),
        P(("band", "exp"), None),
        P(("band", "exp"), None),
        P(("band", "exp"), None),
        P(("band", "exp")),
        P("band"),
    )
    return jax.shard_map(
        on_device, mesh=mesh, in_specs=placed, out_specs=P(("band", "exp"), None), check_vma=False
    )
```

```python
import functools

import jax
import jax.numpy as jnp
from jax import lax
from jax.experimental import pallas as pl
from jax.experimental.pallas import tpu as pltpu
from jax.sharding import PartitionSpec as P

STRIP = 16
TAPS = 15
PATCH_ROWS = 32
LANES = 128
SUB = 8
CHUNKS = 4
QUAD = 4
FAR_ORDER = (2, 1, 3)
NEAR_ORDER = (3, 2, 1)
VMEM_LIMIT = 32 * 1024 * 1024

f32 = jnp.float32
bf16 = jnp.bfloat16


def in_hbm(array):
    return pltpu.with_memory_space_constraint(array, pltpu.HBM)


def swap(block, mask, count):
    return lax.ppermute(block, "exp", [(i, i ^ mask) for i in range(count)])


def call(body, outs, ins, args, scratch=(), flops=0):
    moved = sum(a.size * a.dtype.itemsize for a in args)
    return pl.pallas_call(
        body,
        out_shape=outs,
        in_specs=ins,
        out_specs=jax.tree.map(lambda _: pl.BlockSpec(memory_space=pltpu.VMEM), outs),
        scratch_shapes=scratch,
        compiler_params=pltpu.CompilerParams(vmem_limit_bytes=VMEM_LIMIT),
        cost_estimate=pl.CostEstimate(flops=flops, bytes_accessed=moved, transcendentals=0),
    )(*args)


def lane_dot(left, right):
    return lax.dot_general(left, right, (((1,), (1,)), ((), ())), preferred_element_type=f32)


def parts_of(values):
    high = values.astype(bf16)
    return high, (values - high.astype(f32)).astype(bf16)


def band_tiles(taps):
    half = (TAPS - 1) // 2
    delta = lax.broadcasted_iota(jnp.int32, (LANES, LANES), 0) - lax.broadcasted_iota(
        jnp.int32, (LANES, LANES), 1
    )
    middle = jnp.zeros((LANES, LANES), f32)
    upper = jnp.zeros((SUB, LANES), f32)
    lower = jnp.zeros((SUB, LANES), f32)
    for tap in range(TAPS):
        value = jnp.broadcast_to(taps[:, tap : tap + 1], (1, LANES))
        middle = jnp.where(delta == tap - half, value, middle)
        if tap > half:
            upper = jnp.where(delta[:SUB] == tap - half - LANES, value, upper)
        if tap < half:
            lower = jnp.where(delta[LANES - SUB :] == tap - half + LANES, value, lower)
    rest = jnp.zeros((LANES - SUB, LANES), f32)
    return {
        0: middle,
        -1: jnp.concatenate([rest, lower], axis=0),
        1: jnp.concatenate([upper, rest], axis=0),
    }


def weights_body(
    owner, taps, patch, prow, exposure, col_warp, row_warp,
    ring_ref, own_ref, first_ref, band, cols, rows_ref, select_ref, lines_ref, blocks_ref,
    owner_ref, taps_ref, patch_ref, prow_ref, first_rows, last_rows, sems,
):
    height, width = exposure.shape
    nb = width // LANES
    count = owner_ref.shape[0]
    moves = [
        (taps, taps_ref), (owner, owner_ref), (patch, patch_ref), (prow, prow_ref),
        (col_warp, cols),
        (exposure.at[pl.ds(0, STRIP)], first_rows),
        (exposure.at[pl.ds(height - STRIP, STRIP)], last_rows),
        (row_warp, rows_ref),
    ]
    copies = [pltpu.make_async_copy(*move, sems.at[i]) for i, move in enumerate(moves)]
    for i in (0, 1, 2, 3, 7, 5, 6, 4):
        copies[i].start()

    copies[0].wait()
    tiles = band_tiles(taps_ref[...].astype(f32))
    tiles = {side: tile.astype(bf16) for side, tile in tiles.items()}
    for i in range(nb):
        for k in range(nb):
            tile = tiles.get(k - i, jnp.zeros((LANES, LANES), bf16))
            band[k * LANES : (k + 1) * LANES, i * LANES : (i + 1) * LANES] = tile

    for copy in copies[1:4]:
        copy.wait()
    me = lax.axis_index("exp")
    patch = patch_ref[...]
    slot = jnp.zeros_like(patch)
    for k in range(count):
        slot = jnp.where(patch == owner_ref[k], place_of(me ^ k, count), slot)
    key = slot * PATCH_ROWS + prow_ref[...]
    slots = lax.broadcasted_iota(jnp.int32, select_ref.shape, 0)
    select_ref[...] = jnp.where(slots == key, 1.0, 0.0).astype(bf16)

    for ref in (ring_ref, own_ref, first_ref, blocks_ref, lines_ref):
        ref[...] = jnp.zeros_like(ref)
    base = own_ref.shape[0]

    copies[5].wait()
    copies[6].wait()
    scale = 1.0 / (STRIP * LANES)
    for b in range(nb):
        at = slice(b * LANES, (b + 1) * LANES)
        means = []
        for ref in (first_rows, last_rows):
            column = jnp.sum(ref[:, at], axis=0, keepdims=True)
            total = jnp.sum(column, axis=1, keepdims=True)
            means.append(jnp.broadcast_to(total * scale, (1, LANES)))
        first, last = means
        own_ref[b : b + 1] = 0.5 * (first + last)
        first_ref[b : b + 1] = first
        ring_ref[b : b + 1] = last

    copies[7].wait()
    partial = rows_ref[:, :LANES].astype(f32)
    for i in range(1, height // LANES):
        partial += rows_ref[:, i * LANES : (i + 1) * LANES].astype(f32)
    ones = jnp.ones((2 * SUB, LANES), bf16)
    high, low = parts_of(partial)
    high, low = parts_of(lane_dot(ones, high) + lane_dot(ones, low))
    line = lax.broadcasted_iota(jnp.int32, high.shape, 0)
    left = jnp.where(line == 0, high.astype(f32), jnp.where(line == 1, low.astype(f32), 1.0))
    found = lane_dot(left.astype(bf16), select_ref[...])
    weight = found[0:1] + found[1:2]
    lines_ref[0:1] = weight
    lines_ref[1:2] = found[2:3]
    for i in range(weight.shape[1] // LANES):
        ring_ref[base + nb * nb + i : base + nb * nb + i + 1] = weight[:, i * LANES : (i + 1) * LANES]

    copies[4].wait()
    heads = {side: jnp.sum(tile.astype(f32), axis=0, keepdims=True) for side, tile in tiles.items()}
    blank = jnp.zeros((1, LANES), f32)
    lines = [
        jnp.concatenate([heads.get(b - k, blank) for k in range(nb)], axis=1) for b in range(nb)
    ]
    lines.append(jnp.zeros((base - nb, width), f32))
    high, low = parts_of(jnp.concatenate(lines, axis=0))
    stacked = jnp.concatenate([high.astype(f32), low.astype(f32)], axis=0).astype(bf16)
    both = jnp.dot(stacked, cols[...], preferred_element_type=f32)
    total = both[:base] + both[base:]
    blocks_ref[...] = total
    for b in range(nb):
        for c in range(nb):
            to = base + b * nb + c
            ring_ref[to : to + 1] = total[b : b + 1, c * LANES : (c + 1) * LANES]


def local_body(
    own_ref, image, band, cols, rows, select, sums_ref, high_ref, low_ref, merged, warped
):
    height, width = image.shape
    nb = width // LANES
    step = height // CHUNKS
    merged[...] = jnp.dot(band[...], cols[...], preferred_element_type=f32).astype(bf16)
    for i in range(CHUNKS):
        at = slice(i * step, (i + 1) * step)
        parts = []
        for b in range(nb):
            piece = image[at, b * LANES : (b + 1) * LANES] - own_ref[b : b + 1]
            parts.append(piece.astype(bf16))
        centred = jnp.concatenate(parts, axis=1)
        warped[at] = jnp.dot(centred, merged[...], preferred_element_type=f32).astype(bf16)
    high, low = parts_of(jnp.dot(rows[...], warped[...], preferred_element_type=f32))
    high_ref[...] = high
    low_ref[...] = low
    far = select[: sums_ref.shape[0]]
    sums_ref[...] = jnp.dot(far, high, preferred_element_type=f32) + jnp.dot(
        far, low, preferred_element_type=f32
    )


def place_of(mask, count):
    other, at = mask & 1, lax.shift_right_logical(mask, 1)
    far = count // 2 - QUAD
    return jnp.where(at < QUAD, 2 * far + other * QUAD + at, other * far + at - QUAD)


def mask_of(place, count):
    far = count // 2 - QUAD
    if place < 2 * far:
        return (place % far + QUAD) * 2 + place // far
    return (place - 2 * far) % QUAD * 2 + (place - 2 * far) // QUAD


def upright(line, start):
    shape = (PATCH_ROWS, LANES)
    wanted = lax.broadcasted_iota(jnp.int32, shape, 1) == start + lax.broadcasted_iota(
        jnp.int32, shape, 0
    )
    return jnp.sum(jnp.where(wanted, line, 0.0), axis=1, keepdims=True)


class Levels:
    def __init__(self, got_ref, first_ref, blocks_ref, lines_ref, count):
        nb = blocks_ref.shape[1] // LANES
        base = first_ref.shape[0]
        self.count, self.lines_ref, self.got_ref = count, lines_ref, got_ref
        self.base = base + nb * nb
        self.own, self.other = [], []
        for c in range(nb):
            own = jnp.zeros((1, LANES), f32)
            other = jnp.zeros((1, LANES), f32)
            for b in range(nb):
                level = 0.5 * got_ref[b : b + 1]
                own += level * blocks_ref[b : b + 1, c * LANES : (c + 1) * LANES]
                at = base + b * nb + c
                other += 0.5 * first_ref[b : b + 1] * got_ref[at : at + 1]
            self.own.append(own)
            self.other.append(other)

    def terms(self, j):
        count, each = self.count, LANES // PATCH_ROWS
        me = lax.axis_index("exp")
        mask = mask_of(j, count)
        sender = lax.rem(me + count - 1, count)
        place = place_of(sender ^ me ^ mask, count)
        at = j // each * LANES
        weight = upright(self.lines_ref[0:1, at : at + LANES], j % each * PATCH_ROWS)
        line = self.got_ref[pl.ds(self.base + place // each, 1)]
        far = upright(line, lax.rem(place, each) * PATCH_ROWS)
        return [weight * own + far * other for own, other in zip(self.own, self.other)]

    def held(self, j):
        each = LANES // PATCH_ROWS
        at = j // each * LANES
        line = jnp.broadcast_to(self.lines_ref[1:2, at : at + LANES], (SUB, LANES))
        start = j % each * PATCH_ROWS
        return pltpu.roll(line, LANES - start, 1) if start else line


def put_block(ref, at, size, sums, levels, place, got=None):
    terms = levels.terms(place)
    for c, term in enumerate(terms):
        to = slice(at * size + c * PATCH_ROWS, at * size + (c + 1) * PATCH_ROWS)
        value = sums[:, c * LANES : (c + 1) * LANES] + term
        ref[to] = value if got is None else value + got[c * PATCH_ROWS : (c + 1) * PATCH_ROWS]
    to = at * size + len(terms) * PATCH_ROWS
    held = levels.held(place)
    ref[to : to + SUB] = held if got is None else held + got[size - SUB :]


def far_send_body(count, got_ref, first_ref, blocks_ref, lines_ref, sums_ref, out_ref):
    far = count // 2 - QUAD
    size = out_ref.shape[0] // far
    levels = Levels(got_ref, first_ref, blocks_ref, lines_ref, count)
    for j in range(far):
        at = (far + j) * PATCH_ROWS
        put_block(out_ref, j, size, sums_ref[at : at + PATCH_ROWS], levels, far + j)


def near_body(
    count, got_ref, first_ref, blocks_ref, lines_ref, select, high, low, send_ref, keep_ref
):
    far = count // 2 - QUAD
    size = send_ref.shape[0] // QUAD
    levels = Levels(got_ref, first_ref, blocks_ref, lines_ref, count)
    near = select[2 * far * PATCH_ROWS :]
    sums = jnp.dot(near, high[...], preferred_element_type=f32) + jnp.dot(
        near, low[...], preferred_element_type=f32
    )
    for part, ref in enumerate((keep_ref, send_ref)):
        for j in range(QUAD):
            at = (part * QUAD + j) * PATCH_ROWS
            place = 2 * far + part * QUAD + j
            put_block(ref, j, size, sums[at : at + PATCH_ROWS], levels, place)


def far_merge_body(
    count, got_ref, first_ref, blocks_ref, lines_ref, sums_ref, half_ref, *out_refs
):
    far = count // 2 - QUAD
    size = half_ref.shape[0] // far
    levels = Levels(got_ref, first_ref, blocks_ref, lines_ref, count)
    for j in range(far):
        at = j * PATCH_ROWS
        got = half_ref[j * size : (j + 1) * size]
        put_block(
            out_refs[j % QUAD], j // QUAD, size, sums_ref[at : at + PATCH_ROWS], levels, j, got
        )


def near_merge_body(keep_ref, got_ref, *out_refs):
    size = out_refs[0].shape[0]
    for j, ref in enumerate(out_refs):
        at = slice(j * size, (j + 1) * size)
        ref[...] = keep_ref[at] + got_ref[at]


def far_body(a_ref, b_ref, c_ref, d_ref, *out_refs):
    size = out_refs[0].shape[0]
    for i, ref in enumerate(out_refs):
        at = slice(i * size, (i + 1) * size)
        ref[...] = (a_ref[at] + b_ref[at]) + (c_ref[at] + d_ref[at])


def final_body(*refs):
    out_ref = refs[-1]
    total = refs[0][...]
    for ref in refs[1:-1]:
        total = total + ref[...]
    nb = out_ref.shape[1] // LANES
    number = jnp.maximum(upright(total[nb * PATCH_ROWS : nb * PATCH_ROWS + 1], 0), 1.0)
    for c in range(nb):
        part = total[c * PATCH_ROWS : (c + 1) * PATCH_ROWS]
        out_ref[:, c * LANES : (c + 1) * LANES] = part / number


def on_device(exposure, psf_taps, col_warp, row_warp, row_patch, row_prow, owner_map):
    height, width = exposure.shape
    out_rows = row_warp.shape[0]
    count = lax.axis_size("exp")
    nb = width // LANES
    slots = count * PATCH_ROWS
    half, high_groups = count // 2, count // (2 * QUAD)
    size = PATCH_ROWS * nb + SUB
    vmem = pl.BlockSpec(memory_space=pltpu.VMEM)
    hbm = pl.BlockSpec(memory_space=pltpu.HBM)

    def shape(*dims):
        return jax.ShapeDtypeStruct(dims, f32)

    tile = shape(-(-nb // SUB) * SUB, LANES)
    ring_rows = tile.shape[0] + nb * nb + slots // LANES
    ring, own, first, band, cols, rows, select, lines, blocks = call(
        weights_body,
        [shape(-(-ring_rows // SUB) * SUB, LANES), tile, tile,
         jax.ShapeDtypeStruct((width, width), bf16), jax.ShapeDtypeStruct(col_warp.shape, bf16),
         jax.ShapeDtypeStruct(row_warp.shape, bf16),
         jax.ShapeDtypeStruct((slots, out_rows), bf16), shape(SUB, slots),
         shape(tile.shape[0], width)],
        [hbm] * 7,
        tuple(in_hbm(array) for array in (
            owner_map, psf_taps, row_patch.reshape(1, out_rows), row_prow.reshape(1, out_rows),
            exposure, col_warp, row_warp,
        )),
        scratch=[
            pltpu.SMEM(owner_map.shape, jnp.int32),
            pltpu.VMEM(psf_taps.shape, bf16),
            pltpu.VMEM((1, out_rows), jnp.int32),
            pltpu.VMEM((1, out_rows), jnp.int32),
            pltpu.VMEM((STRIP, width), f32),
            pltpu.VMEM((STRIP, width), f32),
            pltpu.SemaphoreType.DMA((8,)),
        ],
        flops=2 * width * width * width,
    )
    ring = lax.ppermute(ring, "exp", [(i, (i + 1) % count) for i in range(count)])
    far = half - QUAD
    sums, high, low = call(
        local_body,
        [shape(2 * far * PATCH_ROWS, width)] + [jax.ShapeDtypeStruct((out_rows, width), bf16)] * 2,
        [vmem] * 6, (own, exposure, band, cols, rows, select),
        scratch=[pltpu.VMEM((width, width), bf16), pltpu.VMEM((height, width), bf16)],
        flops=2 * height * width * (width + out_rows) + 4 * slots * out_rows * width,
    )
    common = (ring, first, blocks, lines)
    far_send = call(
        functools.partial(far_send_body, count), shape(far * size, LANES), [vmem] * 5,
        common + (sums,),
    )
    far_got = swap(far_send, 1, count)
    near_send, near_keep = call(
        functools.partial(near_body, count), [shape(QUAD * size, LANES)] * 2, [vmem] * 7,
        common + (select, high, low),
    )
    near_got = swap(near_send, 1, count)
    parts = call(
        functools.partial(far_merge_body, count),
        [shape((high_groups - 1) * size, LANES)] * QUAD, [vmem] * 6, common + (sums, far_got),
    )
    terms = [parts[0]] + [swap(parts[q], 2 * q, count) for q in FAR_ORDER]
    near = call(near_merge_body, [shape(size, LANES)] * QUAD, [vmem] * 2, (near_keep, near_got))
    rest = [near[0]] + [swap(near[q], 2 * q, count) for q in NEAR_ORDER]
    sent = call(far_body, [shape(size, LANES)] * (high_groups - 1), [vmem] * QUAD, terms)
    rest = [swap(sent[h - 1], 2 * QUAD * h, count) for h in range(1, high_groups)] + rest
    return call(final_body, shape(PATCH_ROWS, width), [vmem] * len(rest), tuple(rest))


def solution(mesh):
    placed = (
        P(("band", "exp"), None),
        P(("band", "exp"), None),
        P(("band", "exp"), None),
        P(("band", "exp"), None),
        P(("band", "exp"), None),
        P(("band", "exp")),
        P("band"),
    )
    return jax.shard_map(
        on_device, mesh=mesh, in_specs=placed, out_specs=P(("band", "exp"), None), check_vma=False
    )
```

```python
import functools

import jax
import jax.numpy as jnp
from jax import lax
from jax.experimental import pallas as pl
from jax.experimental.pallas import tpu as pltpu
from jax.sharding import PartitionSpec as P

STRIP = 16
TAPS = 15
PATCH_ROWS = 32
LANES = 128
SUB = 8
CHUNKS = 4
QUAD = 4
SHARED = 9
FAR_ORDER = (2, 1, 3)
HOLD = 4_000_000_000
VMEM_LIMIT = 32 * 1024 * 1024

f32 = jnp.float32
bf16 = jnp.bfloat16


def in_hbm(array):
    return pltpu.with_memory_space_constraint(array, pltpu.HBM)


def swap(block, mask, count):
    return lax.ppermute(block, "exp", [(i, i ^ mask) for i in range(count)])


def call(body, outs, ins, args, scratch=(), flops=0, aliases=(), moved=None):
    if moved is None:
        moved = sum(a.size * a.dtype.itemsize for a in args)
    return pl.pallas_call(
        body,
        out_shape=outs,
        in_specs=ins,
        out_specs=jax.tree.map(lambda _: pl.BlockSpec(memory_space=pltpu.VMEM), outs),
        scratch_shapes=scratch,
        input_output_aliases=dict(aliases),
        compiler_params=pltpu.CompilerParams(vmem_limit_bytes=VMEM_LIMIT),
        cost_estimate=pl.CostEstimate(flops=flops, bytes_accessed=moved, transcendentals=0),
    )(*args)


def lane_dot(left, right):
    return lax.dot_general(left, right, (((1,), (1,)), ((), ())), preferred_element_type=f32)


def parts_of(values):
    high = values.astype(bf16)
    return high, (values - high.astype(f32)).astype(bf16)


def band_tiles(taps):
    half = (TAPS - 1) // 2
    delta = lax.broadcasted_iota(jnp.int32, (LANES, LANES), 0) - lax.broadcasted_iota(
        jnp.int32, (LANES, LANES), 1
    )
    middle = jnp.zeros((LANES, LANES), f32)
    upper = jnp.zeros((SUB, LANES), f32)
    lower = jnp.zeros((SUB, LANES), f32)
    for tap in range(TAPS):
        value = jnp.broadcast_to(taps[:, tap : tap + 1], (1, LANES))
        middle = jnp.where(delta == tap - half, value, middle)
        if tap > half:
            upper = jnp.where(delta[:SUB] == tap - half - LANES, value, upper)
        if tap < half:
            lower = jnp.where(delta[LANES - SUB :] == tap - half + LANES, value, lower)
    rest = jnp.zeros((LANES - SUB, LANES), f32)
    return {
        0: middle,
        -1: jnp.concatenate([rest, lower], axis=0),
        1: jnp.concatenate([upper, rest], axis=0),
    }


def block_sums(messages, cols, blocks_ref):
    rows, width = blocks_ref.shape
    nb = width // LANES
    high, low = parts_of(blocks_ref[...])
    stacked = jnp.concatenate([high.astype(f32), low.astype(f32)], axis=0).astype(bf16)
    both = jnp.dot(stacked, cols[...], preferred_element_type=f32)
    total = both[:rows] + both[rows:]
    blocks_ref[...] = total
    for b in range(nb):
        for c in range(nb):
            to = rows + b * nb + c
            for ref in messages:
                ref[to : to + 1] = total[b : b + 1, c * LANES : (c + 1) * LANES]


def row_sums(messages, rows_ref, select_ref, lines_ref, blocks_ref):
    nb = blocks_ref.shape[1] // LANES
    partial = rows_ref[:, :LANES].astype(f32)
    for i in range(1, rows_ref.shape[1] // LANES):
        partial += rows_ref[:, i * LANES : (i + 1) * LANES].astype(f32)
    ones = jnp.ones((2 * SUB, LANES), bf16)
    high, low = parts_of(partial)
    high, low = parts_of(lane_dot(ones, high) + lane_dot(ones, low))
    line = lax.broadcasted_iota(jnp.int32, high.shape, 0)
    left = jnp.where(line == 0, high.astype(f32), jnp.where(line == 1, low.astype(f32), 1.0))
    found = lane_dot(left.astype(bf16), select_ref[...])
    weight = found[0:1] + found[1:2]
    lines_ref[0:1] = weight
    lines_ref[1:2] = found[2:3]
    base = blocks_ref.shape[0] + nb * nb
    for i in range(weight.shape[1] // LANES):
        for ref in messages:
            ref[base + i : base + i + 1] = weight[:, i * LANES : (i + 1) * LANES]


def weights_body(
    owner, taps, patch, prow, exposure, col_warp, row_warp,
    ring_ref, pair_ref, own_ref, first_ref, band, cols, rows_ref, select_ref, lines_ref,
    blocks_ref, owner_ref, taps_ref, patch_ref, prow_ref, first_rows, last_rows, sems,
):
    height, width = exposure.shape
    nb = width // LANES
    count = owner_ref.shape[0]
    moves = [
        (taps, taps_ref), (owner, owner_ref), (patch, patch_ref), (prow, prow_ref),
        (col_warp, cols),
        (exposure.at[pl.ds(0, STRIP)], first_rows),
        (exposure.at[pl.ds(height - STRIP, STRIP)], last_rows),
        (row_warp, rows_ref),
    ]
    copies = [pltpu.make_async_copy(*move, sems.at[i]) for i, move in enumerate(moves)]
    for copy in copies:
        copy.start()
    for ref in (ring_ref, pair_ref, own_ref, first_ref, lines_ref):
        ref[...] = jnp.zeros_like(ref)

    copies[0].wait()
    tiles = band_tiles(taps_ref[...].astype(f32))
    heads = {side: jnp.sum(tile, axis=0, keepdims=True) for side, tile in tiles.items()}
    blank = jnp.zeros((1, LANES), f32)
    lines = [
        jnp.concatenate([heads.get(b - k, blank) for k in range(nb)], axis=1) for b in range(nb)
    ]
    lines.append(jnp.zeros((blocks_ref.shape[0] - nb, width), f32))
    blocks_ref[...] = jnp.concatenate(lines, axis=0)
    tiles = {side: tile.astype(bf16) for side, tile in tiles.items()}
    for i in range(nb):
        for k in range(nb):
            tile = tiles.get(k - i, jnp.zeros((LANES, LANES), bf16))
            band[k * LANES : (k + 1) * LANES, i * LANES : (i + 1) * LANES] = tile

    for copy in copies[1:4]:
        copy.wait()
    me = lax.axis_index("exp")
    odd = lax.rem(me, 2) == 1
    patch = patch_ref[...]
    slot = jnp.zeros_like(patch)
    for k in range(count):
        slot = jnp.where(patch == owner_ref[k], place_of(me ^ k, count, lax.rem(me, 2)), slot)
    key = slot * PATCH_ROWS + prow_ref[...]
    slots = lax.broadcasted_iota(jnp.int32, select_ref.shape, 0)
    select_ref[...] = jnp.where(slots == key, 1.0, 0.0).astype(bf16)

    copies[5].wait()
    copies[6].wait()
    scale = 1.0 / (STRIP * LANES)
    for b in range(nb):
        at = slice(b * LANES, (b + 1) * LANES)
        means = []
        for ref in (first_rows, last_rows):
            column = jnp.sum(ref[:, at], axis=0, keepdims=True)
            total = jnp.sum(column, axis=1, keepdims=True)
            means.append(jnp.broadcast_to(total * scale, (1, LANES)))
        first, last = means
        own_ref[b : b + 1] = 0.5 * (first + last)
        first_ref[b : b + 1] = first
        pair_ref[b : b + 1] = jnp.where(odd, first, last)
        ring_ref[b : b + 1] = jnp.where(odd, last, 0.0)

    copies[4].wait()

    @pl.when(odd)
    def _():
        block_sums([pair_ref, ring_ref], cols, blocks_ref)

    copies[7].wait()

    @pl.when(odd)
    def _():
        row_sums([pair_ref, ring_ref], rows_ref, select_ref, lines_ref, blocks_ref)


def rest_body(*refs):
    pair_ref, _, _, _, cols, rows_ref, select_ref, lines_ref, blocks_ref = refs[SHARED:]

    @pl.when(lax.rem(lax.axis_index("exp"), 2) == 0)
    def _():
        block_sums([pair_ref], cols, blocks_ref)
        row_sums([pair_ref], rows_ref, select_ref, lines_ref, blocks_ref)


def local_body(
    own_ref, image, band, cols, rows, select, sums_ref, high_ref, low_ref, merged, warped
):
    height, width = image.shape
    nb = width // LANES
    step = height // CHUNKS
    merged[...] = jnp.dot(band[...], cols[...], preferred_element_type=f32).astype(bf16)
    for i in range(CHUNKS):
        at = slice(i * step, (i + 1) * step)
        parts = []
        for b in range(nb):
            piece = image[at, b * LANES : (b + 1) * LANES] - own_ref[b : b + 1]
            parts.append(piece.astype(bf16))
        centred = jnp.concatenate(parts, axis=1)
        warped[at] = jnp.dot(centred, merged[...], preferred_element_type=f32).astype(bf16)
    high, low = parts_of(jnp.dot(rows[...], warped[...], preferred_element_type=f32))
    high_ref[...] = high
    low_ref[...] = low
    far = select[: sums_ref.shape[0]]
    sums_ref[...] = jnp.dot(far, high, preferred_element_type=f32) + jnp.dot(
        far, low, preferred_element_type=f32
    )


def place_of(mask, count, kind):
    other, at = lax.rem(mask, 2), mask // 2
    far = count // 2 - QUAD
    wanted = (kind + other) % 2
    side = (at == 1) | (at == 2)
    taker = jnp.where(side, at - 1, wanted)
    index = jnp.where(side, 2 + (wanted + taker) % 2, jnp.where(at == 0, 0, 1))
    near = 2 * far + (taker + kind) % 2 * QUAD + index
    return jnp.where(at < QUAD, near, other * far + at - QUAD)


def mask_of(place, count):
    kind = lax.rem(lax.axis_index("exp"), 2)
    far = count // 2 - QUAD
    if place < 2 * far:
        return (place % far + QUAD) * 2 + place // far
    part, index = (place - 2 * far) // QUAD, (place - 2 * far) % QUAD
    if index < 2:
        return 3 * index * 2 + part
    return (1 + (kind + part) % 2) * 2 + (part + index) % 2


def upright(line, start):
    shape = (PATCH_ROWS, LANES)
    wanted = lax.broadcasted_iota(jnp.int32, shape, 1) == start + lax.broadcasted_iota(
        jnp.int32, shape, 0
    )
    return jnp.sum(jnp.where(wanted, line, 0.0), axis=1, keepdims=True)


def ring_levels(count, *refs):
    return Levels(lax.rem(lax.axis_index("exp") + count - 1, count), *refs, count)


def pair_levels(count, *refs):
    return Levels(lax.axis_index("exp") ^ 1, *refs, count)


class Levels:
    def __init__(self, sender, got_ref, first_ref, blocks_ref, lines_ref, count):
        nb = blocks_ref.shape[1] // LANES
        base = -(-nb // SUB) * SUB
        self.sender = sender
        self.count, self.lines_ref, self.got_ref = count, lines_ref, got_ref
        self.base = base + nb * nb
        self.own, self.other = [], []
        for c in range(nb):
            own = jnp.zeros((1, LANES), f32)
            other = jnp.zeros((1, LANES), f32)
            for b in range(nb):
                level = 0.5 * got_ref[b : b + 1]
                own += level * blocks_ref[b : b + 1, c * LANES : (c + 1) * LANES]
                at = base + b * nb + c
                other += 0.5 * first_ref[b : b + 1] * got_ref[at : at + 1]
            self.own.append(own)
            self.other.append(other)

    def terms(self, j):
        count, each = self.count, LANES // PATCH_ROWS
        me = lax.axis_index("exp")
        mask = mask_of(j, count)
        place = place_of(self.sender ^ me ^ mask, count, lax.rem(self.sender, 2))
        at = j // each * LANES
        weight = upright(self.lines_ref[0:1, at : at + LANES], j % each * PATCH_ROWS)
        line = self.got_ref[pl.ds(self.base + place // each, 1)]
        far = upright(line, lax.rem(place, each) * PATCH_ROWS)
        return [weight * own + far * other for own, other in zip(self.own, self.other)]

    def held(self, j):
        each = LANES // PATCH_ROWS
        at = j // each * LANES
        line = jnp.broadcast_to(self.lines_ref[1:2, at : at + LANES], (SUB, LANES))
        start = j % each * PATCH_ROWS
        return pltpu.roll(line, LANES - start, 1) if start else line


def put_block(ref, at, size, sums, levels, place, got=None):
    terms = [sum(each[1:], each[0]) for each in zip(*[level.terms(place) for level in levels])]
    for c, term in enumerate(terms):
        to = slice(at * size + c * PATCH_ROWS, at * size + (c + 1) * PATCH_ROWS)
        value = sums[:, c * LANES : (c + 1) * LANES] + term
        ref[to] = value if got is None else value + got[c * PATCH_ROWS : (c + 1) * PATCH_ROWS]
    to = at * size + len(terms) * PATCH_ROWS
    held = levels[0].held(place)
    ref[to : to + SUB] = held if got is None else held + got[size - SUB :]


def far_send_body(
    count, size, got_ref, first_ref, blocks_ref, lines_ref, sums_ref, pair_ref, out_ref
):
    far = count // 2 - QUAD
    levels = [ring_levels(count, got_ref, first_ref, blocks_ref, lines_ref)]
    for j in range(far):
        at = (far + j) * PATCH_ROWS
        put_block(out_ref, j, size, sums_ref[at : at + PATCH_ROWS], levels, far + j)
    out_ref[far * size :] = pair_ref[...]


def near_body(
    count, got_ref, first_ref, blocks_ref, lines_ref, select, high, low, send_ref, keep_ref
):
    far = count // 2 - QUAD
    size = send_ref.shape[0] // QUAD
    levels = [ring_levels(count, got_ref, first_ref, blocks_ref, lines_ref)]
    near = select[2 * far * PATCH_ROWS :]
    sums = jnp.dot(near, high[...], preferred_element_type=f32) + jnp.dot(
        near, low[...], preferred_element_type=f32
    )
    for part, ref in enumerate((keep_ref, send_ref)):
        for j in range(QUAD):
            at = (part * QUAD + j) * PATCH_ROWS
            place = 2 * far + part * QUAD + j
            put_block(ref, j, size, sums[at : at + PATCH_ROWS], levels, place)


def far_merge_body(
    count, size, got_ref, first_ref, blocks_ref, lines_ref, sums_ref, pair_ref, half_ref, *out_refs
):
    far = count // 2 - QUAD
    other = half_ref.at[pl.ds(far * size, pair_ref.shape[0])]
    levels = [
        ring_levels(count, got_ref, first_ref, blocks_ref, lines_ref),
        pair_levels(count, other, pair_ref, blocks_ref, lines_ref),
    ]
    for j in range(far):
        at = j * PATCH_ROWS
        got = half_ref[j * size : (j + 1) * size]
        put_block(
            out_refs[j % QUAD], j // QUAD, size, sums_ref[at : at + PATCH_ROWS], levels, j, got
        )


def near_merge_body(
    count, blocks_ref, lines_ref, pair_ref, half_ref, keep_ref, got_ref, own_ref, across_ref, side_ref
):
    far = count // 2 - QUAD
    size = own_ref.shape[0]
    other = half_ref.at[pl.ds(far * size, pair_ref.shape[0])]
    levels = pair_levels(count, other, pair_ref, blocks_ref, lines_ref)
    for j, (ref, base) in enumerate(
        ((own_ref, 0), (across_ref, 0), (side_ref, 0), (side_ref, size))
    ):
        terms = levels.terms(2 * far + j)
        for c, term in enumerate(terms):
            at = slice(j * size + c * PATCH_ROWS, j * size + (c + 1) * PATCH_ROWS)
            to = slice(base + c * PATCH_ROWS, base + (c + 1) * PATCH_ROWS)
            ref[to] = keep_ref[at] + term + got_ref[at]
        at = slice((j + 1) * size - SUB, (j + 1) * size)
        ref[base + size - SUB : base + size] = keep_ref[at] + got_ref[at]


def second_body(ref, out_ref):
    out_ref[...] = ref[out_ref.shape[0] :]


def far_body(a_ref, b_ref, c_ref, d_ref, *out_refs):
    size = out_refs[0].shape[0]
    for i, ref in enumerate(out_refs):
        at = slice(i * size, (i + 1) * size)
        ref[...] = (a_ref[at] + b_ref[at]) + (c_ref[at] + d_ref[at])


def final_body(*refs):
    out_ref = refs[-1]
    total = refs[0][...]
    for ref in refs[1:-1]:
        total = total + ref[: total.shape[0]]
    nb = out_ref.shape[1] // LANES
    number = jnp.maximum(upright(total[nb * PATCH_ROWS : nb * PATCH_ROWS + 1], 0), 1.0)
    for c in range(nb):
        part = total[c * PATCH_ROWS : (c + 1) * PATCH_ROWS]
        out_ref[:, c * LANES : (c + 1) * LANES] = part / number


def on_device(exposure, psf_taps, col_warp, row_warp, row_patch, row_prow, owner_map):
    height, width = exposure.shape
    out_rows = row_warp.shape[0]
    count = lax.axis_size("exp")
    nb = width // LANES
    slots = count * PATCH_ROWS
    half, high_groups = count // 2, count // (2 * QUAD)
    size = PATCH_ROWS * nb + SUB
    vmem = pl.BlockSpec(memory_space=pltpu.VMEM)
    hbm = pl.BlockSpec(memory_space=pltpu.HBM)

    def shape(*dims):
        return jax.ShapeDtypeStruct(dims, f32)

    tile = shape(-(-nb // SUB) * SUB, LANES)
    far = half - QUAD
    ring_rows = tile.shape[0] + nb * nb + slots // LANES
    message = shape(-(-ring_rows // SUB) * SUB, LANES)
    shared = [
        message, tile, tile, jax.ShapeDtypeStruct((width, width), bf16),
        jax.ShapeDtypeStruct(col_warp.shape, bf16), jax.ShapeDtypeStruct(row_warp.shape, bf16),
        jax.ShapeDtypeStruct((slots, out_rows), bf16), shape(SUB, slots),
        shape(tile.shape[0], width),
    ]
    arrays = tuple(in_hbm(array) for array in (
        owner_map, psf_taps, row_patch.reshape(1, out_rows), row_prow.reshape(1, out_rows),
        exposure, col_warp, row_warp,
    ))
    scratch = [
        pltpu.SMEM(owner_map.shape, jnp.int32),
        pltpu.VMEM(psf_taps.shape, bf16),
        pltpu.VMEM((1, out_rows), jnp.int32),
        pltpu.VMEM((1, out_rows), jnp.int32),
        pltpu.VMEM((STRIP, width), f32),
        pltpu.VMEM((STRIP, width), f32),
        pltpu.SemaphoreType.DMA((8,)),
    ]
    ring, *made = call(weights_body, [message] + shared, [hbm] * 7, arrays, scratch=scratch)
    ring = lax.ppermute(ring, "exp", [(i, (i + 1) % count) for i in range(count)])
    pair, own, first, band, cols, rows, select, lines, blocks = call(
        rest_body, shared, [vmem] * SHARED, tuple(made),
        aliases={i: i for i in range(SHARED)},
    )
    sums, high, low = call(
        local_body,
        [shape(2 * far * PATCH_ROWS, width)] + [jax.ShapeDtypeStruct((out_rows, width), bf16)] * 2,
        [vmem] * 6, (own, exposure, band, cols, rows, select),
        scratch=[pltpu.VMEM((width, width), bf16), pltpu.VMEM((height, width), bf16)],
        flops=2 * height * width * (width + out_rows) + 4 * slots * out_rows * width,
    )
    common = (ring, first, blocks, lines)
    far_send = call(
        functools.partial(far_send_body, count, size),
        shape(far * size + pair.shape[0], LANES), [vmem] * 6, common + (sums, pair),
    )
    far_got = swap(far_send, 1, count)
    near_send, near_keep = call(
        functools.partial(near_body, count), [shape(QUAD * size, LANES)] * 2, [vmem] * 7,
        common + (select, high, low),
    )
    near_got = swap(near_send, 1, count)
    parts = call(
        functools.partial(far_merge_body, count, size),
        [shape((high_groups - 1) * size, LANES)] * QUAD, [vmem] * 7,
        common + (sums, pair, far_got),
    )
    terms = [parts[0]] + [swap(parts[q], 2 * q, count) for q in FAR_ORDER]
    kept, across, side = call(
        functools.partial(near_merge_body, count),
        [shape(size, LANES)] * 2 + [shape(2 * size, LANES)], [vmem] * 6,
        (blocks, lines, pair, far_got, near_keep, near_got),
    )
    across = swap(across, 6, count)
    side = lax.ppermute(side, "exp", [(i, i ^ (4 if i % 2 else 2)) for i in range(count)])
    sent = call(
        far_body, [shape(size, LANES)] * (high_groups - 1), [vmem] * QUAD, terms, flops=HOLD
    )
    sums = [swap(sent[h - 1], 2 * QUAD * h, count) for h in range(1, high_groups)]
    passed = swap(call(second_body, shape(size, LANES), [vmem], (side,)), 1, count)
    rest = (kept, across, side, passed, *sums)
    return call(final_body, shape(PATCH_ROWS, width), [vmem] * len(rest), rest)


def solution(mesh):
    placed = (
        P(("band", "exp"), None),
        P(("band", "exp"), None),
        P(("band", "exp"), None),
        P(("band", "exp"), None),
        P(("band", "exp"), None),
        P(("band", "exp")),
        P("band"),
    )
    return jax.shard_map(
        on_device, mesh=mesh, in_specs=placed, out_specs=P(("band", "exp"), None), check_vma=False
    )
```

```python
import functools

import jax
import jax.numpy as jnp
from jax import lax
from jax.experimental import pallas as pl
from jax.experimental.pallas import tpu as pltpu
from jax.sharding import PartitionSpec as P

STRIP = 16
TAPS = 15
PATCH_ROWS = 32
LANES = 128
SUB = 8
CHUNKS = 4
QUAD = 4
SHARED = 9
FAR_ORDER = (3, 1, 2)
HOLD = 4_000_000_000
VMEM_LIMIT = 32 * 1024 * 1024

f32 = jnp.float32
bf16 = jnp.bfloat16


def in_hbm(array):
    return pltpu.with_memory_space_constraint(array, pltpu.HBM)


def swap(block, mask, count):
    return lax.ppermute(block, "exp", [(i, i ^ mask) for i in range(count)])


def call(body, outs, ins, args, scratch=(), flops=0, aliases=(), moved=None):
    if moved is None:
        moved = sum(a.size * a.dtype.itemsize for a in args)
    return pl.pallas_call(
        body,
        out_shape=outs,
        in_specs=ins,
        out_specs=jax.tree.map(lambda _: pl.BlockSpec(memory_space=pltpu.VMEM), outs),
        scratch_shapes=scratch,
        input_output_aliases=dict(aliases),
        compiler_params=pltpu.CompilerParams(vmem_limit_bytes=VMEM_LIMIT),
        cost_estimate=pl.CostEstimate(flops=flops, bytes_accessed=moved, transcendentals=0),
    )(*args)


def lane_dot(left, right):
    return lax.dot_general(left, right, (((1,), (1,)), ((), ())), preferred_element_type=f32)


def parts_of(values):
    high = values.astype(bf16)
    return high, (values - high.astype(f32)).astype(bf16)


def band_tiles(taps):
    half = (TAPS - 1) // 2
    delta = lax.broadcasted_iota(jnp.int32, (LANES, LANES), 0) - lax.broadcasted_iota(
        jnp.int32, (LANES, LANES), 1
    )
    middle = jnp.zeros((LANES, LANES), f32)
    upper = jnp.zeros((SUB, LANES), f32)
    lower = jnp.zeros((SUB, LANES), f32)
    for tap in range(TAPS):
        value = jnp.broadcast_to(taps[:, tap : tap + 1], (1, LANES))
        middle = jnp.where(delta == tap - half, value, middle)
        if tap > half:
            upper = jnp.where(delta[:SUB] == tap - half - LANES, value, upper)
        if tap < half:
            lower = jnp.where(delta[LANES - SUB :] == tap - half + LANES, value, lower)
    rest = jnp.zeros((LANES - SUB, LANES), f32)
    return {
        0: middle,
        -1: jnp.concatenate([rest, lower], axis=0),
        1: jnp.concatenate([upper, rest], axis=0),
    }


def block_sums(messages, cols, blocks_ref):
    rows, width = blocks_ref.shape
    nb = width // LANES
    high, low = parts_of(blocks_ref[...])
    stacked = jnp.concatenate([high.astype(f32), low.astype(f32)], axis=0).astype(bf16)
    both = jnp.dot(stacked, cols[...], preferred_element_type=f32)
    total = both[:rows] + both[rows:]
    blocks_ref[...] = total
    for b in range(nb):
        for c in range(nb):
            to = rows + b * nb + c
            for ref in messages:
                ref[to : to + 1] = total[b : b + 1, c * LANES : (c + 1) * LANES]


def row_sums(messages, rows_ref, select_ref, lines_ref, blocks_ref):
    nb = blocks_ref.shape[1] // LANES
    partial = rows_ref[:, :LANES].astype(f32)
    for i in range(1, rows_ref.shape[1] // LANES):
        partial += rows_ref[:, i * LANES : (i + 1) * LANES].astype(f32)
    ones = jnp.ones((2 * SUB, LANES), bf16)
    high, low = parts_of(partial)
    high, low = parts_of(lane_dot(ones, high) + lane_dot(ones, low))
    line = lax.broadcasted_iota(jnp.int32, high.shape, 0)
    left = jnp.where(line == 0, high.astype(f32), jnp.where(line == 1, low.astype(f32), 1.0))
    found = lane_dot(left.astype(bf16), select_ref[...])
    weight = found[0:1] + found[1:2]
    lines_ref[0:1] = weight
    lines_ref[1:2] = found[2:3]
    base = blocks_ref.shape[0] + nb * nb
    for i in range(weight.shape[1] // LANES):
        for ref in messages:
            ref[base + i : base + i + 1] = weight[:, i * LANES : (i + 1) * LANES]


def weights_body(
    owner, taps, patch, prow, exposure, col_warp, row_warp,
    ring_ref, pair_ref, own_ref, first_ref, band, cols, rows_ref, select_ref, lines_ref,
    blocks_ref, owner_ref, taps_ref, patch_ref, prow_ref, first_rows, last_rows, sems,
):
    height, width = exposure.shape
    nb = width // LANES
    count = owner_ref.shape[0]
    moves = [
        (taps, taps_ref), (owner, owner_ref), (patch, patch_ref), (prow, prow_ref),
        (col_warp, cols),
        (exposure.at[pl.ds(0, STRIP)], first_rows),
        (exposure.at[pl.ds(height - STRIP, STRIP)], last_rows),
        (row_warp, rows_ref),
    ]
    copies = [pltpu.make_async_copy(*move, sems.at[i]) for i, move in enumerate(moves)]
    for copy in copies:
        copy.start()
    for ref in (ring_ref, pair_ref, own_ref, first_ref, lines_ref):
        ref[...] = jnp.zeros_like(ref)

    copies[0].wait()
    tiles = band_tiles(taps_ref[...].astype(f32))
    heads = {side: jnp.sum(tile, axis=0, keepdims=True) for side, tile in tiles.items()}
    blank = jnp.zeros((1, LANES), f32)
    lines = [
        jnp.concatenate([heads.get(b - k, blank) for k in range(nb)], axis=1) for b in range(nb)
    ]
    lines.append(jnp.zeros((blocks_ref.shape[0] - nb, width), f32))
    blocks_ref[...] = jnp.concatenate(lines, axis=0)
    tiles = {side: tile.astype(bf16) for side, tile in tiles.items()}
    for i in range(nb):
        for k in range(nb):
            tile = tiles.get(k - i, jnp.zeros((LANES, LANES), bf16))
            band[k * LANES : (k + 1) * LANES, i * LANES : (i + 1) * LANES] = tile

    for copy in copies[1:4]:
        copy.wait()
    me = lax.axis_index("exp")
    odd = lax.rem(me, 2) == 1
    patch = patch_ref[...]
    slot = jnp.zeros_like(patch)
    for k in range(count):
        slot = jnp.where(patch == owner_ref[k], place_of(me ^ k, count, lax.rem(me, 2)), slot)
    key = slot * PATCH_ROWS + prow_ref[...]
    slots = lax.broadcasted_iota(jnp.int32, select_ref.shape, 0)
    select_ref[...] = jnp.where(slots == key, 1.0, 0.0).astype(bf16)

    copies[5].wait()
    copies[6].wait()
    scale = 1.0 / (STRIP * LANES)
    for b in range(nb):
        at = slice(b * LANES, (b + 1) * LANES)
        means = []
        for ref in (first_rows, last_rows):
            column = jnp.sum(ref[:, at], axis=0, keepdims=True)
            total = jnp.sum(column, axis=1, keepdims=True)
            means.append(jnp.broadcast_to(total * scale, (1, LANES)))
        first, last = means
        own_ref[b : b + 1] = 0.5 * (first + last)
        first_ref[b : b + 1] = first
        pair_ref[b : b + 1] = jnp.where(odd, first, last)
        ring_ref[b : b + 1] = jnp.where(odd, last, 0.0)

    copies[4].wait()

    @pl.when(odd)
    def _():
        block_sums([pair_ref, ring_ref], cols, blocks_ref)

    copies[7].wait()

    @pl.when(odd)
    def _():
        row_sums([pair_ref, ring_ref], rows_ref, select_ref, lines_ref, blocks_ref)


def rest_body(*refs):
    pair_ref, _, _, _, cols, rows_ref, select_ref, lines_ref, blocks_ref = refs[SHARED:]

    @pl.when(lax.rem(lax.axis_index("exp"), 2) == 0)
    def _():
        block_sums([pair_ref], cols, blocks_ref)
        row_sums([pair_ref], rows_ref, select_ref, lines_ref, blocks_ref)


def local_body(
    own_ref, image, band, cols, rows, select, sums_ref, high_ref, low_ref, merged, warped
):
    height, width = image.shape
    nb = width // LANES
    step = height // CHUNKS
    merged[...] = jnp.dot(band[...], cols[...], preferred_element_type=f32).astype(bf16)
    for i in range(CHUNKS):
        at = slice(i * step, (i + 1) * step)
        parts = []
        for b in range(nb):
            piece = image[at, b * LANES : (b + 1) * LANES] - own_ref[b : b + 1]
            parts.append(piece.astype(bf16))
        centred = jnp.concatenate(parts, axis=1)
        warped[at] = jnp.dot(centred, merged[...], preferred_element_type=f32).astype(bf16)
    high, low = parts_of(jnp.dot(rows[...], warped[...], preferred_element_type=f32))
    high_ref[...] = high
    low_ref[...] = low
    far = select[: sums_ref.shape[0]]
    sums_ref[...] = jnp.dot(far, high, preferred_element_type=f32) + jnp.dot(
        far, low, preferred_element_type=f32
    )


def place_of(mask, count, kind):
    other, at = lax.rem(mask, 2), mask // 2
    far = count // 2 - QUAD
    wanted = (kind + other) % 2
    side = (at == 1) | (at == 2)
    taker = jnp.where(side, at - 1, wanted)
    index = jnp.where(side, 2 + (wanted + taker) % 2, jnp.where(at == 0, 0, 1))
    near = 2 * far + (taker + kind) % 2 * QUAD + index
    return jnp.where(at < QUAD, near, other * far + at - QUAD)


def mask_of(place, count):
    kind = lax.rem(lax.axis_index("exp"), 2)
    far = count // 2 - QUAD
    if place < 2 * far:
        return (place % far + QUAD) * 2 + place // far
    part, index = (place - 2 * far) // QUAD, (place - 2 * far) % QUAD
    if index < 2:
        return 3 * index * 2 + part
    return (1 + (kind + part) % 2) * 2 + (part + index) % 2


def upright(line, start):
    shape = (PATCH_ROWS, LANES)
    wanted = lax.broadcasted_iota(jnp.int32, shape, 1) == start + lax.broadcasted_iota(
        jnp.int32, shape, 0
    )
    return jnp.sum(jnp.where(wanted, line, 0.0), axis=1, keepdims=True)


def ring_levels(count, *refs):
    return Levels(lax.rem(lax.axis_index("exp") + count - 1, count), *refs, count)


def pair_levels(count, *refs):
    return Levels(lax.axis_index("exp") ^ 1, *refs, count)


class Levels:
    def __init__(self, sender, got_ref, first_ref, blocks_ref, lines_ref, count):
        nb = blocks_ref.shape[1] // LANES
        base = -(-nb // SUB) * SUB
        self.sender = sender
        self.count, self.lines_ref, self.got_ref = count, lines_ref, got_ref
        self.base = base + nb * nb
        self.own, self.other = [], []
        for c in range(nb):
            own = jnp.zeros((1, LANES), f32)
            other = jnp.zeros((1, LANES), f32)
            for b in range(nb):
                level = 0.5 * got_ref[b : b + 1]
                own += level * blocks_ref[b : b + 1, c * LANES : (c + 1) * LANES]
                at = base + b * nb + c
                other += 0.5 * first_ref[b : b + 1] * got_ref[at : at + 1]
            self.own.append(own)
            self.other.append(other)

    def terms(self, j):
        count, each = self.count, LANES // PATCH_ROWS
        me = lax.axis_index("exp")
        mask = mask_of(j, count)
        place = place_of(self.sender ^ me ^ mask, count, lax.rem(self.sender, 2))
        at = j // each * LANES
        weight = upright(self.lines_ref[0:1, at : at + LANES], j % each * PATCH_ROWS)
        line = self.got_ref[pl.ds(self.base + place // each, 1)]
        far = upright(line, lax.rem(place, each) * PATCH_ROWS)
        return [weight * own + far * other for own, other in zip(self.own, self.other)]

    def held(self, j):
        each = LANES // PATCH_ROWS
        at = j // each * LANES
        line = jnp.broadcast_to(self.lines_ref[1:2, at : at + LANES], (SUB, LANES))
        start = j % each * PATCH_ROWS
        return pltpu.roll(line, LANES - start, 1) if start else line


def put_block(ref, at, size, sums, levels, place, got=None):
    terms = [sum(each[1:], each[0]) for each in zip(*[level.terms(place) for level in levels])]
    for c, term in enumerate(terms):
        to = slice(at * size + c * PATCH_ROWS, at * size + (c + 1) * PATCH_ROWS)
        value = sums[:, c * LANES : (c + 1) * LANES] + term
        ref[to] = value if got is None else value + got[c * PATCH_ROWS : (c + 1) * PATCH_ROWS]
    to = at * size + len(terms) * PATCH_ROWS
    held = levels[0].held(place)
    ref[to : to + SUB] = held if got is None else held + got[size - SUB :]


def far_send_body(
    count, size, got_ref, first_ref, blocks_ref, lines_ref, sums_ref, pair_ref, out_ref
):
    far = count // 2 - QUAD
    levels = [ring_levels(count, got_ref, first_ref, blocks_ref, lines_ref)]
    for j in range(far):
        at = (far + j) * PATCH_ROWS
        put_block(out_ref, j, size, sums_ref[at : at + PATCH_ROWS], levels, far + j)
    out_ref[far * size :] = pair_ref[...]


def near_body(
    count, got_ref, first_ref, blocks_ref, lines_ref, select, high, low, send_ref, keep_ref
):
    far = count // 2 - QUAD
    size = send_ref.shape[0] // QUAD
    levels = [ring_levels(count, got_ref, first_ref, blocks_ref, lines_ref)]
    near = select[2 * far * PATCH_ROWS :]
    sums = jnp.dot(near, high[...], preferred_element_type=f32) + jnp.dot(
        near, low[...], preferred_element_type=f32
    )
    for part, ref in enumerate((keep_ref, send_ref)):
        for j in range(QUAD):
            at = (part * QUAD + j) * PATCH_ROWS
            place = 2 * far + part * QUAD + j
            put_block(ref, j, size, sums[at : at + PATCH_ROWS], levels, place)


def far_keep_body(count, size, got_ref, first_ref, blocks_ref, lines_ref, sums_ref, out_ref):
    levels = [ring_levels(count, got_ref, first_ref, blocks_ref, lines_ref)]
    for j in range(count // 2 - QUAD):
        at = j * PATCH_ROWS
        put_block(out_ref, j, size, sums_ref[at : at + PATCH_ROWS], levels, j)


def far_merge_body(count, size, blocks_ref, lines_ref, pair_ref, keep_ref, half_ref, *out_refs):
    far = count // 2 - QUAD
    other = half_ref.at[pl.ds(far * size, pair_ref.shape[0])]
    levels = pair_levels(count, other, pair_ref, blocks_ref, lines_ref)
    for j in range(far):
        ref, base = out_refs[j % QUAD], j // QUAD * size
        for c, term in enumerate(levels.terms(j)):
            at = slice(j * size + c * PATCH_ROWS, j * size + (c + 1) * PATCH_ROWS)
            to = slice(base + c * PATCH_ROWS, base + (c + 1) * PATCH_ROWS)
            ref[to] = keep_ref[at] + term + half_ref[at]
        at = slice((j + 1) * size - SUB, (j + 1) * size)
        ref[base + size - SUB : base + size] = keep_ref[at] + half_ref[at]


def near_merge_body(
    count, blocks_ref, lines_ref, pair_ref, half_ref, keep_ref, got_ref, own_ref, across_ref, side_ref
):
    far = count // 2 - QUAD
    size = own_ref.shape[0]
    other = half_ref.at[pl.ds(far * size, pair_ref.shape[0])]
    levels = pair_levels(count, other, pair_ref, blocks_ref, lines_ref)
    for j, (ref, base) in enumerate(
        ((own_ref, 0), (across_ref, 0), (side_ref, 0), (side_ref, size))
    ):
        terms = levels.terms(2 * far + j)
        for c, term in enumerate(terms):
            at = slice(j * size + c * PATCH_ROWS, j * size + (c + 1) * PATCH_ROWS)
            to = slice(base + c * PATCH_ROWS, base + (c + 1) * PATCH_ROWS)
            ref[to] = keep_ref[at] + term + got_ref[at]
        at = slice((j + 1) * size - SUB, (j + 1) * size)
        ref[base + size - SUB : base + size] = keep_ref[at] + got_ref[at]


def second_body(ref, out_ref):
    out_ref[...] = ref[out_ref.shape[0] :]


def far_body(a_ref, b_ref, c_ref, d_ref, *out_refs):
    size = out_refs[0].shape[0]
    for i, ref in enumerate(out_refs):
        at = slice(i * size, (i + 1) * size)
        ref[...] = (a_ref[at] + b_ref[at]) + (c_ref[at] + d_ref[at])


def final_body(*refs):
    out_ref = refs[-1]
    total = refs[0][...]
    for ref in refs[1:-1]:
        total = total + ref[: total.shape[0]]
    nb = out_ref.shape[1] // LANES
    number = jnp.maximum(upright(total[nb * PATCH_ROWS : nb * PATCH_ROWS + 1], 0), 1.0)
    for c in range(nb):
        part = total[c * PATCH_ROWS : (c + 1) * PATCH_ROWS]
        out_ref[:, c * LANES : (c + 1) * LANES] = part / number


def on_device(exposure, psf_taps, col_warp, row_warp, row_patch, row_prow, owner_map):
    height, width = exposure.shape
    out_rows = row_warp.shape[0]
    count = lax.axis_size("exp")
    nb = width // LANES
    slots = count * PATCH_ROWS
    half, high_groups = count // 2, count // (2 * QUAD)
    size = PATCH_ROWS * nb + SUB
    vmem = pl.BlockSpec(memory_space=pltpu.VMEM)
    hbm = pl.BlockSpec(memory_space=pltpu.HBM)

    def shape(*dims):
        return jax.ShapeDtypeStruct(dims, f32)

    tile = shape(-(-nb // SUB) * SUB, LANES)
    far = half - QUAD
    ring_rows = tile.shape[0] + nb * nb + slots // LANES
    message = shape(-(-ring_rows // SUB) * SUB, LANES)
    shared = [
        message, tile, tile, jax.ShapeDtypeStruct((width, width), bf16),
        jax.ShapeDtypeStruct(col_warp.shape, bf16), jax.ShapeDtypeStruct(row_warp.shape, bf16),
        jax.ShapeDtypeStruct((slots, out_rows), bf16), shape(SUB, slots),
        shape(tile.shape[0], width),
    ]
    arrays = tuple(in_hbm(array) for array in (
        owner_map, psf_taps, row_patch.reshape(1, out_rows), row_prow.reshape(1, out_rows),
        exposure, col_warp, row_warp,
    ))
    scratch = [
        pltpu.SMEM(owner_map.shape, jnp.int32),
        pltpu.VMEM(psf_taps.shape, bf16),
        pltpu.VMEM((1, out_rows), jnp.int32),
        pltpu.VMEM((1, out_rows), jnp.int32),
        pltpu.VMEM((STRIP, width), f32),
        pltpu.VMEM((STRIP, width), f32),
        pltpu.SemaphoreType.DMA((8,)),
    ]
    ring, *made = call(weights_body, [message] + shared, [hbm] * 7, arrays, scratch=scratch)
    ring = lax.ppermute(ring, "exp", [(i, (i + 1) % count) for i in range(count)])
    pair, own, first, band, cols, rows, select, lines, blocks = call(
        rest_body, shared, [vmem] * SHARED, tuple(made),
        aliases={i: i for i in range(SHARED)},
    )
    sums, high, low = call(
        local_body,
        [shape(2 * far * PATCH_ROWS, width)] + [jax.ShapeDtypeStruct((out_rows, width), bf16)] * 2,
        [vmem] * 6, (own, exposure, band, cols, rows, select),
        scratch=[pltpu.VMEM((width, width), bf16), pltpu.VMEM((height, width), bf16)],
        flops=2 * height * width * (width + out_rows) + 4 * slots * out_rows * width,
    )
    common = (ring, first, blocks, lines)
    far_send = call(
        functools.partial(far_send_body, count, size),
        shape(far * size + pair.shape[0], LANES), [vmem] * 6, common + (sums, pair),
    )
    far_send, kept_sums = lax.optimization_barrier((far_send, sums))
    far_got = swap(far_send, 1, count)
    far_keep = call(
        functools.partial(far_keep_body, count, size), shape(far * size, LANES), [vmem] * 5,
        common + (kept_sums,),
    )
    near_send, near_keep = call(
        functools.partial(near_body, count), [shape(QUAD * size, LANES)] * 2, [vmem] * 7,
        common + (select, high, low),
    )
    near_got = swap(near_send, 1, count)
    parts = call(
        functools.partial(far_merge_body, count, size),
        [shape((high_groups - 1) * size, LANES)] * QUAD, [vmem] * 5,
        (blocks, lines, pair, far_keep, far_got),
    )
    terms = [parts[0]] + [swap(parts[q], 2 * q, count) for q in FAR_ORDER]
    kept, across, side = call(
        functools.partial(near_merge_body, count),
        [shape(size, LANES)] * 2 + [shape(2 * size, LANES)], [vmem] * 6,
        (blocks, lines, pair, far_got, near_keep, near_got),
    )
    across, terms[1] = lax.optimization_barrier((across, terms[1]))
    across = swap(across, 6, count)
    side = lax.ppermute(side, "exp", [(i, i ^ (4 if i % 2 else 2)) for i in range(count)])
    sent = call(
        far_body, [shape(size, LANES)] * (high_groups - 1), [vmem] * QUAD, terms, flops=HOLD
    )
    sums = [swap(sent[h - 1], 2 * QUAD * h, count) for h in range(1, high_groups)]
    passed = swap(call(second_body, shape(size, LANES), [vmem], (side,)), 1, count)
    rest = (kept, across, side, passed, *sums)
    return call(final_body, shape(PATCH_ROWS, width), [vmem] * len(rest), rest)


def solution(mesh):
    placed = (
        P(("band", "exp"), None),
        P(("band", "exp"), None),
        P(("band", "exp"), None),
        P(("band", "exp"), None),
        P(("band", "exp"), None),
        P(("band", "exp")),
        P("band"),
    )
    return jax.shard_map(
        on_device, mesh=mesh, in_specs=placed, out_specs=P(("band", "exp"), None), check_vma=False
    )
```

```python
import functools

import jax
import jax.numpy as jnp
from jax import lax
from jax.experimental import pallas as pl
from jax.experimental.pallas import tpu as pltpu
from jax.sharding import PartitionSpec as P

STRIP = 16
TAPS = 15
PATCH_ROWS = 32
LANES = 128
SUB = 8
CHUNKS = 4
QUAD = 4
SHARED = 9
FAR_ORDER = (3, 1, 2)
HOLD = 4_000_000_000
VMEM_LIMIT = 32 * 1024 * 1024

f32 = jnp.float32
bf16 = jnp.bfloat16


def in_hbm(array):
    return pltpu.with_memory_space_constraint(array, pltpu.HBM)


def swap(block, mask, count):
    return lax.ppermute(block, "exp", [(i, i ^ mask) for i in range(count)])


def call(body, outs, ins, args, scratch=(), flops=0, aliases=(), moved=None):
    if moved is None:
        moved = sum(a.size * a.dtype.itemsize for a in args)
    return pl.pallas_call(
        body,
        out_shape=outs,
        in_specs=ins,
        out_specs=jax.tree.map(lambda _: pl.BlockSpec(memory_space=pltpu.VMEM), outs),
        scratch_shapes=scratch,
        input_output_aliases=dict(aliases),
        compiler_params=pltpu.CompilerParams(vmem_limit_bytes=VMEM_LIMIT),
        cost_estimate=pl.CostEstimate(flops=flops, bytes_accessed=moved, transcendentals=0),
    )(*args)


def lane_dot(left, right):
    return lax.dot_general(left, right, (((1,), (1,)), ((), ())), preferred_element_type=f32)


def parts_of(values):
    high = values.astype(bf16)
    return high, (values - high.astype(f32)).astype(bf16)


def band_tiles(taps):
    half = (TAPS - 1) // 2
    delta = lax.broadcasted_iota(jnp.int32, (LANES, LANES), 0) - lax.broadcasted_iota(
        jnp.int32, (LANES, LANES), 1
    )
    middle = jnp.zeros((LANES, LANES), f32)
    upper = jnp.zeros((SUB, LANES), f32)
    lower = jnp.zeros((SUB, LANES), f32)
    for tap in range(TAPS):
        value = jnp.broadcast_to(taps[:, tap : tap + 1], (1, LANES))
        middle = jnp.where(delta == tap - half, value, middle)
        if tap > half:
            upper = jnp.where(delta[:SUB] == tap - half - LANES, value, upper)
        if tap < half:
            lower = jnp.where(delta[LANES - SUB :] == tap - half + LANES, value, lower)
    rest = jnp.zeros((LANES - SUB, LANES), f32)
    return {
        0: middle,
        -1: jnp.concatenate([rest, lower], axis=0),
        1: jnp.concatenate([upper, rest], axis=0),
    }


def block_sums(messages, cols, blocks_ref):
    rows, width = blocks_ref.shape
    nb = width // LANES
    high, low = parts_of(blocks_ref[...])
    stacked = jnp.concatenate([high.astype(f32), low.astype(f32)], axis=0).astype(bf16)
    both = jnp.dot(stacked, cols[...], preferred_element_type=f32)
    total = both[:rows] + both[rows:]
    blocks_ref[...] = total
    for b in range(nb):
        for c in range(nb):
            to = rows + b * nb + c
            for ref in messages:
                ref[to : to + 1] = total[b : b + 1, c * LANES : (c + 1) * LANES]


def row_sums(messages, rows_ref, select_ref, lines_ref, blocks_ref):
    nb = blocks_ref.shape[1] // LANES
    partial = rows_ref[:, :LANES].astype(f32)
    for i in range(1, rows_ref.shape[1] // LANES):
        partial += rows_ref[:, i * LANES : (i + 1) * LANES].astype(f32)
    ones = jnp.ones((2 * SUB, LANES), bf16)
    high, low = parts_of(partial)
    high, low = parts_of(lane_dot(ones, high) + lane_dot(ones, low))
    line = lax.broadcasted_iota(jnp.int32, high.shape, 0)
    left = jnp.where(line == 0, high.astype(f32), jnp.where(line == 1, low.astype(f32), 1.0))
    found = lane_dot(left.astype(bf16), select_ref[...])
    weight = found[0:1] + found[1:2]
    lines_ref[0:1] = weight
    lines_ref[1:2] = found[2:3]
    base = blocks_ref.shape[0] + nb * nb
    for i in range(weight.shape[1] // LANES):
        for ref in messages:
            ref[base + i : base + i + 1] = weight[:, i * LANES : (i + 1) * LANES]


def weights_body(
    owner, taps, patch, prow, exposure, col_warp, row_warp,
    ring_ref, pair_ref, own_ref, first_ref, band, cols, rows_ref, select_ref, lines_ref,
    blocks_ref, owner_ref, taps_ref, patch_ref, prow_ref, first_rows, last_rows, sems,
):
    height, width = exposure.shape
    nb = width // LANES
    count = owner_ref.shape[0]
    moves = [
        (taps, taps_ref), (owner, owner_ref), (patch, patch_ref), (prow, prow_ref),
        (col_warp, cols),
        (exposure.at[pl.ds(0, STRIP)], first_rows),
        (exposure.at[pl.ds(height - STRIP, STRIP)], last_rows),
        (row_warp, rows_ref),
    ]
    copies = [pltpu.make_async_copy(*move, sems.at[i]) for i, move in enumerate(moves)]
    for copy in copies:
        copy.start()
    for ref in (ring_ref, pair_ref, own_ref, first_ref, lines_ref):
        ref[...] = jnp.zeros_like(ref)

    copies[0].wait()
    tiles = band_tiles(taps_ref[...].astype(f32))
    heads = {side: jnp.sum(tile, axis=0, keepdims=True) for side, tile in tiles.items()}
    blank = jnp.zeros((1, LANES), f32)
    lines = [
        jnp.concatenate([heads.get(b - k, blank) for k in range(nb)], axis=1) for b in range(nb)
    ]
    lines.append(jnp.zeros((blocks_ref.shape[0] - nb, width), f32))
    blocks_ref[...] = jnp.concatenate(lines, axis=0)
    tiles = {side: tile.astype(bf16) for side, tile in tiles.items()}
    for i in range(nb):
        for k in range(nb):
            tile = tiles.get(k - i, jnp.zeros((LANES, LANES), bf16))
            band[k * LANES : (k + 1) * LANES, i * LANES : (i + 1) * LANES] = tile

    for copy in copies[1:4]:
        copy.wait()
    me = lax.axis_index("exp")
    odd = lax.rem(me, 2) == 1
    patch = patch_ref[...]
    slot = jnp.zeros_like(patch)
    for k in range(count):
        slot = jnp.where(patch == owner_ref[k], place_of(me ^ k, count, lax.rem(me, 2)), slot)
    key = slot * PATCH_ROWS + prow_ref[...]
    slots = lax.broadcasted_iota(jnp.int32, select_ref.shape, 0)
    select_ref[...] = jnp.where(slots == key, 1.0, 0.0).astype(bf16)

    copies[5].wait()
    copies[6].wait()
    scale = 1.0 / (STRIP * LANES)
    for b in range(nb):
        at = slice(b * LANES, (b + 1) * LANES)
        means = []
        for ref in (first_rows, last_rows):
            column = jnp.sum(ref[:, at], axis=0, keepdims=True)
            total = jnp.sum(column, axis=1, keepdims=True)
            means.append(jnp.broadcast_to(total * scale, (1, LANES)))
        first, last = means
        own_ref[b : b + 1] = 0.5 * (first + last)
        first_ref[b : b + 1] = first
        pair_ref[b : b + 1] = jnp.where(odd, first, last)
        ring_ref[b : b + 1] = jnp.where(odd, last, 0.0)

    copies[4].wait()

    @pl.when(odd)
    def _():
        block_sums([pair_ref, ring_ref], cols, blocks_ref)

    copies[7].wait()

    @pl.when(odd)
    def _():
        row_sums([pair_ref, ring_ref], rows_ref, select_ref, lines_ref, blocks_ref)


def rest_body(*refs):
    pair_ref, _, _, _, cols, rows_ref, select_ref, lines_ref, blocks_ref = refs[SHARED:]

    @pl.when(lax.rem(lax.axis_index("exp"), 2) == 0)
    def _():
        block_sums([pair_ref], cols, blocks_ref)
        row_sums([pair_ref], rows_ref, select_ref, lines_ref, blocks_ref)


def local_body(
    own_ref, image, band, cols, rows, select, sums_ref, high_ref, low_ref, merged, warped
):
    height, width = image.shape
    nb = width // LANES
    step = height // CHUNKS
    merged[...] = jnp.dot(band[...], cols[...], preferred_element_type=f32).astype(bf16)
    for i in range(CHUNKS):
        at = slice(i * step, (i + 1) * step)
        parts = []
        for b in range(nb):
            piece = image[at, b * LANES : (b + 1) * LANES] - own_ref[b : b + 1]
            parts.append(piece.astype(bf16))
        centred = jnp.concatenate(parts, axis=1)
        warped[at] = jnp.dot(centred, merged[...], preferred_element_type=f32).astype(bf16)
    high, low = parts_of(jnp.dot(rows[...], warped[...], preferred_element_type=f32))
    high_ref[...] = high
    low_ref[...] = low
    far = select[: sums_ref.shape[0]]
    sums_ref[...] = jnp.dot(far, high, preferred_element_type=f32) + jnp.dot(
        far, low, preferred_element_type=f32
    )


def place_of(mask, count, kind):
    other, at = lax.rem(mask, 2), mask // 2
    far = count // 2 - QUAD
    wanted = (kind + other) % 2
    side = (at == 1) | (at == 2)
    taker = jnp.where(side, 2 - at, wanted)
    index = jnp.where(side, 2 + (wanted + taker) % 2, jnp.where(at == 0, 0, 1))
    near = 2 * far + (taker + kind) % 2 * QUAD + index
    return jnp.where(at < QUAD, near, other * far + at - QUAD)


def mask_of(place, count):
    kind = lax.rem(lax.axis_index("exp"), 2)
    far = count // 2 - QUAD
    if place < 2 * far:
        return (place % far + QUAD) * 2 + place // far
    part, index = (place - 2 * far) // QUAD, (place - 2 * far) % QUAD
    if index < 2:
        return 3 * index * 2 + part
    return (2 - (kind + part) % 2) * 2 + (part + index) % 2


def upright(line, start):
    shape = (PATCH_ROWS, LANES)
    wanted = lax.broadcasted_iota(jnp.int32, shape, 1) == start + lax.broadcasted_iota(
        jnp.int32, shape, 0
    )
    return jnp.sum(jnp.where(wanted, line, 0.0), axis=1, keepdims=True)


def ring_levels(count, *refs):
    return Levels(lax.rem(lax.axis_index("exp") + count - 1, count), *refs, count)


def pair_levels(count, *refs):
    return Levels(lax.axis_index("exp") ^ 1, *refs, count)


class Levels:
    def __init__(self, sender, got_ref, first_ref, blocks_ref, lines_ref, count):
        nb = blocks_ref.shape[1] // LANES
        base = -(-nb // SUB) * SUB
        self.sender = sender
        self.count, self.lines_ref, self.got_ref = count, lines_ref, got_ref
        self.base = base + nb * nb
        self.own, self.other = [], []
        for c in range(nb):
            own = jnp.zeros((1, LANES), f32)
            other = jnp.zeros((1, LANES), f32)
            for b in range(nb):
                level = 0.5 * got_ref[b : b + 1]
                own += level * blocks_ref[b : b + 1, c * LANES : (c + 1) * LANES]
                at = base + b * nb + c
                other += 0.5 * first_ref[b : b + 1] * got_ref[at : at + 1]
            self.own.append(own)
            self.other.append(other)

    def terms(self, j):
        count, each = self.count, LANES // PATCH_ROWS
        me = lax.axis_index("exp")
        mask = mask_of(j, count)
        place = place_of(self.sender ^ me ^ mask, count, lax.rem(self.sender, 2))
        at = j // each * LANES
        weight = upright(self.lines_ref[0:1, at : at + LANES], j % each * PATCH_ROWS)
        line = self.got_ref[pl.ds(self.base + place // each, 1)]
        far = upright(line, lax.rem(place, each) * PATCH_ROWS)
        return [weight * own + far * other for own, other in zip(self.own, self.other)]

    def held(self, j):
        each = LANES // PATCH_ROWS
        at = j // each * LANES
        line = jnp.broadcast_to(self.lines_ref[1:2, at : at + LANES], (SUB, LANES))
        start = j % each * PATCH_ROWS
        return pltpu.roll(line, LANES - start, 1) if start else line


def put_block(ref, at, size, sums, levels, place, got=None):
    terms = [sum(each[1:], each[0]) for each in zip(*[level.terms(place) for level in levels])]
    for c, term in enumerate(terms):
        to = slice(at * size + c * PATCH_ROWS, at * size + (c + 1) * PATCH_ROWS)
        value = sums[:, c * LANES : (c + 1) * LANES] + term
        ref[to] = value if got is None else value + got[c * PATCH_ROWS : (c + 1) * PATCH_ROWS]
    to = at * size + len(terms) * PATCH_ROWS
    held = levels[0].held(place)
    ref[to : to + SUB] = held if got is None else held + got[size - SUB :]


def far_send_body(
    count, size, got_ref, first_ref, blocks_ref, lines_ref, sums_ref, pair_ref, out_ref
):
    far = count // 2 - QUAD
    levels = [ring_levels(count, got_ref, first_ref, blocks_ref, lines_ref)]
    for j in range(far):
        at = (far + j) * PATCH_ROWS
        put_block(out_ref, j, size, sums_ref[at : at + PATCH_ROWS], levels, far + j)
    out_ref[far * size :] = pair_ref[...]


def near_body(
    count, got_ref, first_ref, blocks_ref, lines_ref, select, high, low, send_ref, keep_ref
):
    far = count // 2 - QUAD
    size = send_ref.shape[0] // QUAD
    levels = [ring_levels(count, got_ref, first_ref, blocks_ref, lines_ref)]
    near = select[2 * far * PATCH_ROWS :]
    sums = jnp.dot(near, high[...], preferred_element_type=f32) + jnp.dot(
        near, low[...], preferred_element_type=f32
    )
    for part, ref in enumerate((keep_ref, send_ref)):
        for j in range(QUAD):
            at = (part * QUAD + j) * PATCH_ROWS
            place = 2 * far + part * QUAD + j
            put_block(ref, j, size, sums[at : at + PATCH_ROWS], levels, place)


def far_keep_body(count, size, got_ref, first_ref, blocks_ref, lines_ref, sums_ref, out_ref):
    levels = [ring_levels(count, got_ref, first_ref, blocks_ref, lines_ref)]
    for j in range(count // 2 - QUAD):
        at = j * PATCH_ROWS
        put_block(out_ref, j, size, sums_ref[at : at + PATCH_ROWS], levels, j)


def far_merge_body(count, size, blocks_ref, lines_ref, pair_ref, keep_ref, half_ref, *out_refs):
    far = count // 2 - QUAD
    other = half_ref.at[pl.ds(far * size, pair_ref.shape[0])]
    levels = pair_levels(count, other, pair_ref, blocks_ref, lines_ref)
    for j in range(far):
        ref, base = out_refs[j % QUAD], j // QUAD * size
        for c, term in enumerate(levels.terms(j)):
            at = slice(j * size + c * PATCH_ROWS, j * size + (c + 1) * PATCH_ROWS)
            to = slice(base + c * PATCH_ROWS, base + (c + 1) * PATCH_ROWS)
            ref[to] = keep_ref[at] + term + half_ref[at]
        at = slice((j + 1) * size - SUB, (j + 1) * size)
        ref[base + size - SUB : base + size] = keep_ref[at] + half_ref[at]


def near_merge_body(
    count, blocks_ref, lines_ref, pair_ref, half_ref, keep_ref, got_ref, own_ref, across_ref, side_ref
):
    far = count // 2 - QUAD
    size = own_ref.shape[0]
    other = half_ref.at[pl.ds(far * size, pair_ref.shape[0])]
    levels = pair_levels(count, other, pair_ref, blocks_ref, lines_ref)
    for j, (ref, base) in enumerate(
        ((own_ref, 0), (across_ref, 0), (side_ref, 0), (side_ref, size))
    ):
        terms = levels.terms(2 * far + j)
        for c, term in enumerate(terms):
            at = slice(j * size + c * PATCH_ROWS, j * size + (c + 1) * PATCH_ROWS)
            to = slice(base + c * PATCH_ROWS, base + (c + 1) * PATCH_ROWS)
            ref[to] = keep_ref[at] + term + got_ref[at]
        at = slice((j + 1) * size - SUB, (j + 1) * size)
        ref[base + size - SUB : base + size] = keep_ref[at] + got_ref[at]


def second_body(ref, out_ref):
    out_ref[...] = ref[out_ref.shape[0] :]


def far_body(a_ref, b_ref, c_ref, d_ref, *out_refs):
    size = out_refs[0].shape[0]
    for i, ref in enumerate(out_refs):
        at = slice(i * size, (i + 1) * size)
        ref[...] = (a_ref[at] + b_ref[at]) + (c_ref[at] + d_ref[at])


def final_body(*refs):
    out_ref = refs[-1]
    total = refs[0][...]
    for ref in refs[1:-1]:
        total = total + ref[: total.shape[0]]
    nb = out_ref.shape[1] // LANES
    number = jnp.maximum(upright(total[nb * PATCH_ROWS : nb * PATCH_ROWS + 1], 0), 1.0)
    for c in range(nb):
        part = total[c * PATCH_ROWS : (c + 1) * PATCH_ROWS]
        out_ref[:, c * LANES : (c + 1) * LANES] = part / number


def on_device(exposure, psf_taps, col_warp, row_warp, row_patch, row_prow, owner_map):
    height, width = exposure.shape
    out_rows = row_warp.shape[0]
    count = lax.axis_size("exp")
    nb = width // LANES
    slots = count * PATCH_ROWS
    half, high_groups = count // 2, count // (2 * QUAD)
    size = PATCH_ROWS * nb + SUB
    vmem = pl.BlockSpec(memory_space=pltpu.VMEM)
    hbm = pl.BlockSpec(memory_space=pltpu.HBM)

    def shape(*dims):
        return jax.ShapeDtypeStruct(dims, f32)

    tile = shape(-(-nb // SUB) * SUB, LANES)
    far = half - QUAD
    ring_rows = tile.shape[0] + nb * nb + slots // LANES
    message = shape(-(-ring_rows // SUB) * SUB, LANES)
    shared = [
        message, tile, tile, jax.ShapeDtypeStruct((width, width), bf16),
        jax.ShapeDtypeStruct(col_warp.shape, bf16), jax.ShapeDtypeStruct(row_warp.shape, bf16),
        jax.ShapeDtypeStruct((slots, out_rows), bf16), shape(SUB, slots),
        shape(tile.shape[0], width),
    ]
    arrays = tuple(in_hbm(array) for array in (
        owner_map, psf_taps, row_patch.reshape(1, out_rows), row_prow.reshape(1, out_rows),
        exposure, col_warp, row_warp,
    ))
    scratch = [
        pltpu.SMEM(owner_map.shape, jnp.int32),
        pltpu.VMEM(psf_taps.shape, bf16),
        pltpu.VMEM((1, out_rows), jnp.int32),
        pltpu.VMEM((1, out_rows), jnp.int32),
        pltpu.VMEM((STRIP, width), f32),
        pltpu.VMEM((STRIP, width), f32),
        pltpu.SemaphoreType.DMA((8,)),
    ]
    ring, *made = call(weights_body, [message] + shared, [hbm] * 7, arrays, scratch=scratch)
    ring = lax.ppermute(ring, "exp", [(i, (i + 1) % count) for i in range(count)])
    pair, own, first, band, cols, rows, select, lines, blocks = call(
        rest_body, shared, [vmem] * SHARED, tuple(made),
        aliases={i: i for i in range(SHARED)},
    )
    sums, high, low = call(
        local_body,
        [shape(2 * far * PATCH_ROWS, width)] + [jax.ShapeDtypeStruct((out_rows, width), bf16)] * 2,
        [vmem] * 6, (own, exposure, band, cols, rows, select),
        scratch=[pltpu.VMEM((width, width), bf16), pltpu.VMEM((height, width), bf16)],
        flops=2 * height * width * (width + out_rows) + 4 * slots * out_rows * width,
    )
    common = (ring, first, blocks, lines)
    far_send = call(
        functools.partial(far_send_body, count, size),
        shape(far * size + pair.shape[0], LANES), [vmem] * 6, common + (sums, pair),
    )
    far_send, kept_sums = lax.optimization_barrier((far_send, sums))
    far_got = swap(far_send, 1, count)
    far_keep = call(
        functools.partial(far_keep_body, count, size), shape(far * size, LANES), [vmem] * 5,
        common + (kept_sums,),
    )
    near_send, near_keep = call(
        functools.partial(near_body, count), [shape(QUAD * size, LANES)] * 2, [vmem] * 7,
        common + (select, high, low),
    )
    near_got = swap(near_send, 1, count)
    parts = call(
        functools.partial(far_merge_body, count, size),
        [shape((high_groups - 1) * size, LANES)] * QUAD, [vmem] * 5,
        (blocks, lines, pair, far_keep, far_got),
    )
    terms = [parts[0]] + [swap(parts[q], 2 * q, count) for q in FAR_ORDER]
    kept, across, side = call(
        functools.partial(near_merge_body, count),
        [shape(size, LANES)] * 2 + [shape(2 * size, LANES)], [vmem] * 6,
        (blocks, lines, pair, far_got, near_keep, near_got),
    )
    across, terms[1] = lax.optimization_barrier((across, terms[1]))
    across = swap(across, 6, count)
    side = lax.ppermute(side, "exp", [(i, i ^ (2 if i % 2 else 4)) for i in range(count)])
    sent = call(
        far_body, [shape(size, LANES)] * (high_groups - 1), [vmem] * QUAD, terms, flops=HOLD
    )
    sums = [swap(sent[h - 1], 2 * QUAD * h, count) for h in range(1, high_groups)]
    passed = swap(call(second_body, shape(size, LANES), [vmem], (side,)), 1, count)
    rest = (kept, across, side, passed, *sums)
    return call(final_body, shape(PATCH_ROWS, width), [vmem] * len(rest), rest)


def solution(mesh):
    placed = (
        P(("band", "exp"), None),
        P(("band", "exp"), None),
        P(("band", "exp"), None),
        P(("band", "exp"), None),
        P(("band", "exp"), None),
        P(("band", "exp")),
        P("band"),
    )
    return jax.shard_map(
        on_device, mesh=mesh, in_specs=placed, out_specs=P(("band", "exp"), None), check_vma=False
    )
```
